128 devices in a mesh: shard: 16 (over z, y), ctx: 2 (over x_hi), tp: 4 (over x_lo, core).
Axes of the slice: x: 4 (x_hi: 2, x_lo: 2; x = x_hi * 2 + x_lo), y: 4, z: 4, core: 2. Of those that a mesh axis runs over, the one named last changes fastest.
Arguments:
- hidden_in: bfloat16 [16, 1024, 1024], P('shard', 'ctx'), may hold values from -6 to 6
- w_query: bfloat16 [1024, 1024], P('shard', 'tp'), may hold values from -0.1875 to 0.1875
- key_weight: bfloat16 [1024, 512], P('shard', 'tp'), may hold values from -0.1875 to 0.1875
- value_weight: bfloat16 [1024, 512], P('shard', 'tp'), may hold values from -0.1875 to 0.1875
- w_out: bfloat16 [1024, 1024], P('tp', 'shard'), may hold values from -1.5 to 1.5
- w_gate: bfloat16 [1024, 4608], P('shard', 'tp'), may hold values from -0.1875 to 0.1875
- w_up: bfloat16 [1024, 4608], P('shard', 'tp'), may hold values from -0.1875 to 0.1875
- w_down: bfloat16 [4608, 1024], P('tp', 'shard'), may hold values from -0.09375 to 0.09375
- norm_gains: bfloat16 [2, 1024], P(None, 'shard'), may hold values from 0.099609375 to 1.8984375
- head_gains: bfloat16 [2, 64], P(None, 'shard'), may hold values from 0.099609375 to 1.8984375
- cotangent: bfloat16 [16, 1024, 1024], P('shard', 'ctx'), may hold values from -6 to 6
Outputs:
- block_out: bfloat16 [16, 1024, 1024], P('shard', 'ctx')
- grad_in: float32 [16, 1024, 1024], P('shard', 'ctx')
- grad_w_query: float32 [1024, 1024], P('shard', 'tp')
- grad_w_key: float32 [1024, 512], P('shard', 'tp')
- grad_w_value: float32 [1024, 512], P('shard', 'tp')
- grad_w_out: float32 [1024, 1024], P('tp', 'shard')
- grad_w_gate: float32 [1024, 4608], P('shard', 'tp')
- grad_w_up: float32 [1024, 4608], P('shard', 'tp')
- grad_w_down: float32 [4608, 1024], P('tp', 'shard')
- grad_norm_gains: float32 [2, 1024], P(None, 'shard')
- grad_head_gains: float32 [2, 64], P(None, 'shard')
The draws below stay inside these ranges and needn't reach their ends.
All inputs are finite; a program needn't handle non-finite values.
Results may differ from the reference program's by a relative error of at most 0.033.
Values may be sent and summed in bfloat16 or wider, within the bound.
A program may use at most 128 MiB of HBM per device.

```python
import math
import jax
import jax.numpy as jnp
from jax import lax

MODEL_WIDTH = 1024
QUERY_HEADS = 16
KEY_VALUE_HEADS = 8
HEAD_SIZE = 64
FF = 4608
SEQ = 1024
SEQS = 16


def with_spikes(drawn, rng, source, target, blocks, factor):
    def block_of(position):
        return (jnp.arange(drawn.shape[position]) // (drawn.shape[position] // blocks)).reshape((-1,) + (1,) * (drawn.ndim - 1 - position))

    first = jax.random.permutation(rng, blocks)[block_of(target)]
    far = (block_of(target) + blocks // 2) % blocks
    return jnp.where((block_of(source) == first) | (block_of(source) == far), factor * drawn, drawn)


def levels(key, dims, split, smallest, top_value):
    factor_of = 1.0
    for axis_at, parts in split:
        draws = jax.random.uniform(jax.random.fold_in(jax.random.fold_in(key, 6), axis_at), (parts,), jnp.float32, smallest / len(split), top_value / len(split))
        factor_of = factor_of * jnp.repeat(jnp.exp(draws), dims[axis_at] // parts).reshape((-1,) + (1,) * (len(dims) - 1 - axis_at))
    return factor_of


def gaussian(rng, shape, scale, reach, split=(), held_as=jnp.bfloat16):
    values = jax.random.normal(rng, shape, jnp.float32) * scale
    if len(split) > 0:
        values = levels(rng, shape, split, -0.22, 0.18) * values
    return jnp.clip(values, min=-reach, max=reach).astype(held_as)


def gaussian_with(own_key, dims, spread, most, shards, heavy, kind=jnp.bfloat16):
    entries = spread * jax.random.normal(own_key, dims, jnp.float32)
    if shards:
        entries = entries * levels(own_key, dims, shards, -0.22, 0.18)
    return jnp.clip(with_spikes(entries, jax.random.fold_in(own_key, 3), *heavy), -most, most).astype(kind)


def setup_inputs(seed: int = 0) -> dict:
    seeds = jax.random.split(jax.random.key(seed), 12)
    hidden_in = gaussian(seeds[0], (SEQS, SEQ, MODEL_WIDTH), 1.0, 6.0, ((0, 16), (1, 2)))
    w_query = gaussian(seeds[1], (MODEL_WIDTH, QUERY_HEADS * HEAD_SIZE), MODEL_WIDTH ** -0.5, 0.1875, ((0, 16), (1, 4)))
    key_weight = gaussian(seeds[2], (MODEL_WIDTH, KEY_VALUE_HEADS * HEAD_SIZE), MODEL_WIDTH ** -0.5, 0.1875, ((0, 16), (1, 4)))
    value_weight = gaussian(seeds[3], (MODEL_WIDTH, KEY_VALUE_HEADS * HEAD_SIZE), MODEL_WIDTH ** -0.5, 0.1875, ((0, 16), (1, 4)))
    w_out = gaussian(seeds[4], (QUERY_HEADS * HEAD_SIZE, MODEL_WIDTH), QUERY_HEADS ** -0.5, 1.5, ((0, 4), (1, 16)))
    w_gate = gaussian(seeds[5], (MODEL_WIDTH, FF), MODEL_WIDTH ** -0.5, 0.1875, ((0, 16), (1, 4)))
    w_up = gaussian(seeds[6], (MODEL_WIDTH, FF), MODEL_WIDTH ** -0.5, 0.1875, ((0, 16), (1, 4)))
    w_down = gaussian(seeds[7], (FF, MODEL_WIDTH), FF ** -0.5, 0.09375, ((0, 4), (1, 16)))
    norm_gains = jnp.clip(1.0 + 0.18 * jax.random.normal(seeds[8], (2, MODEL_WIDTH), jnp.float32), 0.099609375, 1.8984375).astype(jnp.bfloat16)
    head_gains = jnp.clip(1.0 + 0.18 * jax.random.normal(seeds[9], (2, HEAD_SIZE), jnp.float32), 0.099609375, 1.8984375).astype(jnp.bfloat16)
    cotangent = gaussian_with(seeds[10], (SEQS, SEQ, MODEL_WIDTH), 1.0, 6.0, ((0, 16), (1, 2)), (1, 2, 2, 2.0))
    return {"hidden_in": hidden_in, "w_query": w_query, "key_weight": key_weight, "value_weight": value_weight, "w_out": w_out, "w_gate": w_gate, "w_up": w_up, "w_down": w_down, "norm_gains": norm_gains, "head_gains": head_gains, "cotangent": cotangent}


EPS = 1e-05
THETA = 1000000.0

@jax.custom_vjp
def reduced_precision(v):
    return lax.optimization_barrier(v.astype(jnp.bfloat16)).astype(jnp.float32)

@jax.custom_vjp
def reduced_backward(v):
    return v

def low_keep(v):
    return (reduced_precision(v), None)

def low_pass(kept, grad):
    return (grad,)

def back_keep(v):
    return (v, None)

def back_low(kept, grad):
    return (reduced_precision(grad),)
reduced_precision.defvjp(low_keep, low_pass)
reduced_backward.defvjp(back_keep, back_low)

def rms_rows(vector):
    return vector * lax.rsqrt(lax.optimization_barrier(jnp.mean(vector * vector, axis=-1, keepdims=True)) + EPS)

def tables(positions, width):
    half_width = width // 2
    frequency = THETA ** (-jnp.arange(half_width, dtype=jnp.float32) / half_width)
    angles = positions[:, None] * frequency[None, :]
    return (jnp.cos(angles), jnp.sin(angles))

def rotate(vector, cosine, sine_table):
    half_width = vector.shape[-1] // 2
    first_half = vector[..., :half_width]
    second = vector[..., half_width:]
    cos_b = cosine[:, None, :]
    sin_b = sine_table[:, None, :]
    return jnp.concatenate([first_half * cos_b - second * sin_b, second * cos_b + first_half * sin_b], axis=-1)

def block_forward(tokens, w_query, key_weight, value_weight, w_out, w_gate, w_up, w_down, norm_gains, head_gains):
    exact_matmul = lax.Precision.HIGHEST
    token_length = tokens.shape[0]
    normalized_input = reduced_precision(rms_rows(tokens) * norm_gains[0])
    query_raw = reduced_backward(jnp.dot(normalized_input, w_query, precision=exact_matmul)).reshape(token_length, QUERY_HEADS, HEAD_SIZE)
    key_unrotated = reduced_backward(jnp.dot(normalized_input, key_weight, precision=exact_matmul)).reshape(token_length, KEY_VALUE_HEADS, HEAD_SIZE)
    value_rows = reduced_backward(reduced_precision(jnp.dot(normalized_input, value_weight, precision=exact_matmul))).reshape(token_length, KEY_VALUE_HEADS, HEAD_SIZE)
    positions = jnp.arange(token_length, dtype=jnp.float32)
    cosine, sine_table = tables(positions, HEAD_SIZE)
    query_heads_rows = reduced_backward(reduced_precision(rotate(rms_rows(query_raw) * head_gains[0], cosine, sine_table)))
    query_heads_rows = query_heads_rows.reshape(token_length, KEY_VALUE_HEADS, QUERY_HEADS // KEY_VALUE_HEADS, HEAD_SIZE)
    keys_all = reduced_backward(reduced_precision(rotate(rms_rows(key_unrotated) * head_gains[1], cosine, sine_table)))
    block_rows = math.gcd(token_length, 512)

    def attend(begin_row):
        query_rows = lax.dynamic_slice_in_dim(query_heads_rows, begin_row, block_rows, 0)
        scores = reduced_backward(jnp.einsum('qkgd,skd->kgqs', query_rows, keys_all, precision=exact_matmul) * 0.125)
        query_pos = begin_row + jnp.arange(block_rows, dtype=jnp.int32)
        key_pos = jnp.arange(token_length, dtype=jnp.int32)
        visible = key_pos[None, :] <= query_pos[:, None]
        attn_probs = jax.nn.softmax(jnp.where(visible, scores, -1e+30), axis=-1)
        return jnp.einsum('kgqs,skd->qkgd', reduced_precision(attn_probs), value_rows, precision=exact_matmul)
    starts = jnp.arange(0, token_length, block_rows, dtype=jnp.int32)
    blocks = lax.map(jax.checkpoint(attend), starts)
    attended = reduced_backward(reduced_precision(blocks.reshape(token_length, QUERY_HEADS * HEAD_SIZE)))
    residual = tokens + reduced_backward(jnp.dot(attended, w_out, precision=exact_matmul))
    mlp_in = reduced_precision(rms_rows(residual) * norm_gains[1])
    gate_proj = reduced_backward(jnp.dot(mlp_in, w_gate, precision=exact_matmul))
    up_proj = reduced_backward(jnp.dot(mlp_in, w_up, precision=exact_matmul))
    hidden_act = reduced_precision(jax.nn.silu(gate_proj) * up_proj)
    return residual + reduced_backward(jnp.dot(hidden_act, w_down, precision=exact_matmul))

def reference(hidden_in, w_query, key_weight, value_weight, w_out, w_gate, w_up, w_down, norm_gains, head_gains, cotangent):
    params = tuple((weight.astype(jnp.float32) for weight in (w_query, key_weight, value_weight, w_out, w_gate, w_up, w_down, norm_gains, head_gains)))

    def one_sequence(totals, inputs_now):
        tokens, grad_top = inputs_now
        block_val, pullback = jax.vjp(block_forward, tokens.astype(jnp.float32), *params)
        gradients = pullback(grad_top.astype(jnp.float32))
        totals = tuple((total + part for total, part in zip(totals, gradients[1:])))
        return (totals, (block_val.astype(jnp.bfloat16), gradients[0]))
    initial = tuple((jnp.zeros(weight.shape, jnp.float32) for weight in params))
    totals, (outputs, grads_in) = lax.scan(one_sequence, initial, (hidden_in, cotangent))
    return (outputs, grads_in, totals[0], totals[1], totals[2], totals[3], totals[4], totals[5], totals[6], totals[7], totals[8])
```

```python
import functools

import jax
import jax.numpy as jnp
from jax import lax
from jax.experimental import pallas as pl
from jax.experimental.pallas import tpu as pltpu
from jax.sharding import PartitionSpec as P

HEAD_SIZE = 64
EPS = 1e-05
THETA = 1000000.0
MESH = pl.DeviceIdType.MESH
VMEM_LIMIT = 56 * 1024 * 1024
HALF = 32
QUARTER = 16
SHARD_ROWS = 64


def ring_place():
    me = lax.axis_index("shard")
    return me // 4, lax.rem(me, 4)


def shard_at(z, y):
    return {"shard": lax.rem(z + 4, 4) * 4 + lax.rem(y + 4, 4)}


def greet(partners):
    barrier = pltpu.get_barrier_semaphore()
    for partner in partners:
        pl.semaphore_signal(barrier, inc=1, device_id=partner, device_id_type=MESH)
    pl.semaphore_wait(barrier, len(partners))


def remote(src, dst, send_sem, recv_sem, target):
    return pltpu.make_async_remote_copy(
        src_ref=src,
        dst_ref=dst,
        send_sem=send_sem,
        recv_sem=recv_sem,
        device_id=target,
        device_id_type=MESH,
    )


def torus_partners():
    z, y = ring_place()
    return [shard_at(z, y + 1), shard_at(z, y - 1), shard_at(z + 1, y), shard_at(z - 1, y)]


class Gather:

    def __init__(self, full, columns, send_sem, recv_sem, base):
        self.full = full
        self.columns = columns
        self.send_sem = send_sem
        self.recv_sem = recv_sem
        self.base = base
        self.z, self.y = ring_place()

    def rows(self, half, first, second, part):
        z, y = (self.z + second, self.y + first) if half == 0 else (self.z + first, self.y + second)
        block = lax.rem(z + 4, 4) * 4 + lax.rem(y + 4, 4)
        start = block * SHARD_ROWS + half * HALF + (QUARTER if part == 2 else 0)
        count = HALF if part == 0 else QUARTER
        lo, hi = self.columns
        return self.full.at[pl.ds(pl.multiple_of(start, QUARTER), count), lo:hi]

    def target(self, half, first, second):
        if half == 0:
            return shard_at(self.z + second, self.y + first)
        return shard_at(self.z + first, self.y + second)

    def copy(self, half, k, landed=False):
        if k < 4:
            step = (1, -1)[k % 2]
            if k < 2:
                sent, got = (0, 0, 0), (-step, 0, 0)
            else:
                sent, got = (-step, 0, 1 + k % 2), (-2 * step, 0, 1 + k % 2)
            target = (step, 0)
        else:
            j, kind = (k - 4) // 4, (k - 4) % 4
            offset = (0, -1, 1, 2)[j]
            step = (1, -1)[kind % 2]
            if kind < 2:
                sent, got = (offset, 0, 0), (offset, -step, 0)
            else:
                sent, got = (offset, -step, 1 + kind % 2), (offset, -2 * step, 1 + kind % 2)
            target = (0, step)
        index = self.base + half * 20 + k
        rows = self.rows(half, *(got if landed else sent))
        return remote(
            rows, rows, self.send_sem.at[index], self.recv_sem.at[index], self.target(half, *target)
        )

    def start(self, *ks):
        for k in ks:
            for half in (0, 1):
                self.copy(half, k).start()

    def arrived(self, *ks):
        for k in ks:
            for half in (0, 1):
                self.copy(half, k, True).wait_recv()

    def step(self, n):
        if n == 0:
            self.start(0, 1, 4, 5)
        elif n == 1:
            self.arrived(0)
            self.start(2, 8, 9)
            self.arrived(1)
            self.start(3, 12, 13)
        elif n == 2:
            self.arrived(4)
            self.start(6)
            self.arrived(5)
            self.start(7)
        elif n == 3:
            self.arrived(2, 3)
            self.start(16, 17)
        elif n == 4:
            for k in (8, 9, 12, 13, 16, 17):
                self.arrived(k)
                self.start(k + 2)
        elif n == 5:
            self.arrived(6, 7, 10, 11, 14, 15, 18, 19)

    def finish(self):
        for k in range(20):
            for half in (0, 1):
                self.copy(half, k).wait_send()


def gather_kernel(chunks, own_ref, full_ref, send_sem, recv_sem):
    greet(torus_partners())
    me = lax.axis_index("shard")
    full_ref[pl.ds(pl.multiple_of(me * SHARD_ROWS, SHARD_ROWS), SHARD_ROWS), :] = own_ref[...]
    parts = [Gather(full_ref, chunk, send_sem, recv_sem, 40 * i) for i, chunk in enumerate(chunks)]
    for n in range(6):
        for part in parts:
            part.step(n)
    for part in parts:
        part.finish()


def gather_weights(own, chunks):
    width = own.shape[1]
    return pl.pallas_call(
        functools.partial(gather_kernel, chunks),
        out_shape=jax.ShapeDtypeStruct((16 * SHARD_ROWS, width), own.dtype),
        in_specs=[pl.BlockSpec(memory_space=pltpu.VMEM)],
        out_specs=pl.BlockSpec(memory_space=pltpu.VMEM),
        scratch_shapes=[
            pltpu.SemaphoreType.DMA((40 * len(chunks),)),
            pltpu.SemaphoreType.DMA((40 * len(chunks),)),
        ],
        compiler_params=pltpu.CompilerParams(
            collective_id=0, has_side_effects=True, vmem_limit_bytes=VMEM_LIMIT
        ),
        name="gather_weights",
    )(own)


class Scatter:

    def __init__(self, part, landing, columns, send_sem, recv_sem, base):
        self.part = part
        self.landing = landing
        self.columns = columns
        self.send_sem = send_sem
        self.recv_sem = recv_sem
        self.base = base
        self.z, self.y = ring_place()

    def place(self, half, first, second):
        if half == 0:
            z, y = self.z + second, self.y + first
        else:
            z, y = self.z + first, self.y + second
        return lax.rem(z + 4, 4) * 4 + lax.rem(y + 4, 4)

    def rows(self, half, first, second, part):
        start = self.place(half, first, second) * SHARD_ROWS + half * HALF
        start = start + (QUARTER if part == 2 else 0)
        count = HALF if part == 0 else QUARTER
        lo, hi = self.columns
        return self.part.at[pl.ds(pl.multiple_of(start, QUARTER), count), lo:hi]

    def slot(self, half, j, kind):
        start = ((half * 5 + j) * 2) * 48 + (kind % 2) * 48 + (QUARTER if kind >= 2 else 0)
        count = HALF if kind >= 2 else QUARTER
        lo, hi = self.columns
        return self.landing.at[start : start + count, lo:hi]

    def copy(self, half, j, kind):
        step = (1, -1)[kind % 2]
        if kind < 2:
            along, part = 2, 1 + kind % 2
        else:
            along, part = step, 0
        if j < 4:
            offset = (2, -1, 1, 0)[j]
            src = self.rows(half, offset, along, part)
            target = {"shard": self.place(half, 0, step)}
        else:
            src = self.rows(half, along, 0, part)
            target = {"shard": self.place(half, step, 0)}
        index = self.base + (half * 5 + j) * 4 + kind
        return remote(src, self.slot(half, j, kind), self.send_sem.at[index], self.recv_sem.at[index], target)

    def add(self, half, target, *slots):
        total = target[...].astype(jnp.float32)
        for slot in slots:
            total = total + slot[...].astype(jnp.float32)
        target[...] = total.astype(jnp.bfloat16)

    def first(self, j):
        for half in (0, 1):
            for kind in (0, 1):
                self.copy(half, j, kind).start()

    def second(self, j):
        for kind in (0, 1):
            for half in (0, 1):
                self.copy(half, j, kind).wait_recv()
                step = (1, -1)[kind]
                if j < 4:
                    target = self.rows(half, (2, -1, 1, 0)[j], step, 1 + kind)
                else:
                    target = self.rows(half, step, 0, 1 + kind)
                self.add(half, target, self.slot(half, j, kind))
                self.copy(half, j, kind + 2).start()

    def third(self, j):
        for half in (0, 1):
            self.copy(half, j, 2).wait_recv()
            self.copy(half, j, 3).wait_recv()
            target = self.rows(half, (2, -1, 1, 0)[j] if j < 4 else 0, 0, 0)
            self.add(half, target, self.slot(half, j, 2), self.slot(half, j, 3))

    def finish(self):
        for half in (0, 1):
            for j in range(5):
                for kind in range(4):
                    self.copy(half, j, kind).wait_send()


def scatter_kernel(chunks, part_ref, out_ref, work, landing, other, send_sem, recv_sem, ctx_send, ctx_recv):
    ctx_peer = {"ctx": 1 - lax.axis_index("ctx")}
    greet(torus_partners() + [ctx_peer])
    me = lax.axis_index("shard")
    mine = pl.ds(pl.multiple_of(me * SHARD_ROWS, SHARD_ROWS), SHARD_ROWS)
    fetch = pltpu.make_async_copy(part_ref, work, ctx_send.at[len(chunks)])
    fetch.start()
    fetch.wait()
    parts = [Scatter(work, landing, chunk, send_sem, recv_sem, 40 * i) for i, chunk in enumerate(chunks)]

    def to_peer(i):
        lo, hi = chunks[i]
        return remote(work.at[mine, lo:hi], other.at[:, lo:hi], ctx_send.at[i], ctx_recv.at[i], ctx_peer)

    for part in parts:
        for j in range(4):
            part.first(j)
    for i, part in enumerate(parts):
        for j in range(4):
            part.second(j)
        for j in range(3):
            part.third(j)
        part.first(4)
        part.third(3)
        part.second(4)
    for i, part in enumerate(parts):
        part.third(4)
        to_peer(i).start()
    for i, part in enumerate(parts):
        to_peer(i).wait()
        lo, hi = chunks[i]
        out_ref[:, lo:hi] = work[mine, lo:hi].astype(jnp.float32) + other[:, lo:hi].astype(jnp.float32)
        part.finish()


def scatter_gradients(part, chunks):
    width = part.shape[1]
    return pl.pallas_call(
        functools.partial(scatter_kernel, chunks),
        out_shape=jax.ShapeDtypeStruct((SHARD_ROWS, width), jnp.float32),
        in_specs=[pl.BlockSpec(memory_space=pl.ANY)],
        out_specs=pl.BlockSpec(memory_space=pltpu.VMEM),
        scratch_shapes=[
            pltpu.VMEM((16 * SHARD_ROWS, width), jnp.bfloat16),
            pltpu.VMEM((960, width), jnp.bfloat16),
            pltpu.VMEM((SHARD_ROWS, width), jnp.bfloat16),
            pltpu.SemaphoreType.DMA((40 * len(chunks),)),
            pltpu.SemaphoreType.DMA((40 * len(chunks),)),
            pltpu.SemaphoreType.DMA((len(chunks) + 1,)),
            pltpu.SemaphoreType.DMA((len(chunks),)),
        ],
        compiler_params=pltpu.CompilerParams(
            collective_id=1, has_side_effects=True, vmem_limit_bytes=VMEM_LIMIT
        ),
        name="scatter_gradients",
    )(part)


def tp_place():
    me = lax.axis_index("tp")
    return me // 2, lax.rem(me, 2)


def tp_sum_kernel(part_ref, out_ref, landed, folded, send_sem, recv_sem):
    chip, core = tp_place()
    size = part_ref.shape[0] // 4
    next_core = {"tp": chip * 2 + 1 - core}
    next_chip = {"tp": (1 - chip) * 2 + core}
    greet([next_core, next_chip])

    def block(chip_at, core_at):
        return pl.ds(pl.multiple_of((chip_at * 2 + core_at) * size, QUARTER), size)

    across = [
        remote(
            part_ref.at[block(chip_at, 1 - core)],
            landed.at[slot],
            send_sem.at[slot],
            recv_sem.at[slot],
            next_core,
        )
        for slot, chip_at in ((0, 1 - chip), (1, chip))
    ]
    for copy in across:
        copy.start()
    across[0].wait_recv()
    folded[0] = (
        part_ref[block(1 - chip, core), :].astype(jnp.float32) + landed[0].astype(jnp.float32)
    ).astype(jnp.bfloat16)
    over = remote(folded.at[0], landed.at[2], send_sem.at[2], recv_sem.at[2], next_chip)
    over.start()
    across[1].wait_recv()
    over.wait_recv()
    mine = block(chip, core)
    out_ref[mine, :] = (
        part_ref[mine, :].astype(jnp.float32)
        + landed[1].astype(jnp.float32)
        + landed[2].astype(jnp.float32)
    ).astype(jnp.bfloat16)
    back_chip = remote(out_ref.at[mine], out_ref.at[mine], send_sem.at[3], recv_sem.at[3], next_chip)
    back_core = remote(out_ref.at[mine], out_ref.at[mine], send_sem.at[4], recv_sem.at[4], next_core)
    back_chip.start()
    back_core.start()
    theirs = block(1 - chip, core)
    back_chip.wait_recv()
    relay = remote(out_ref.at[theirs], out_ref.at[theirs], send_sem.at[5], recv_sem.at[5], next_core)
    relay.start()
    back_core.wait_recv()
    relay.wait_recv()
    for copy in across + [over, back_chip, back_core, relay]:
        copy.wait_send()


def tp_total(part, collective_id):
    rows, width = part.shape
    size = rows // 4
    return pl.pallas_call(
        tp_sum_kernel,
        out_shape=jax.ShapeDtypeStruct((rows, width), jnp.bfloat16),
        in_specs=[pl.BlockSpec(memory_space=pltpu.VMEM)],
        out_specs=pl.BlockSpec(memory_space=pltpu.VMEM),
        scratch_shapes=[
            pltpu.VMEM((3, size, width), jnp.bfloat16),
            pltpu.VMEM((1, size, width), jnp.bfloat16),
            pltpu.SemaphoreType.DMA((6,)),
            pltpu.SemaphoreType.DMA((6,)),
        ],
        compiler_params=pltpu.CompilerParams(
            collective_id=collective_id, has_side_effects=True, vmem_limit_bytes=VMEM_LIMIT
        ),
        name=f"tp_total_{collective_id}",
    )(part)


def swap_kernel(own_ref, other_ref, send_sem, recv_sem):
    peer = {"ctx": 1 - lax.axis_index("ctx")}
    greet([peer])
    copy = remote(own_ref, other_ref, send_sem, recv_sem, peer)
    copy.start()
    copy.wait()


def ctx_swap(own, collective_id):
    return pl.pallas_call(
        swap_kernel,
        out_shape=jax.ShapeDtypeStruct(own.shape, own.dtype),
        in_specs=[pl.BlockSpec(memory_space=pltpu.VMEM)],
        out_specs=pl.BlockSpec(memory_space=pltpu.VMEM),
        scratch_shapes=[pltpu.SemaphoreType.DMA, pltpu.SemaphoreType.DMA],
        compiler_params=pltpu.CompilerParams(
            collective_id=collective_id, has_side_effects=True, vmem_limit_bytes=VMEM_LIMIT
        ),
        name=f"ctx_swap_{collective_id}",
    )(own)


def rms_rows(vector):
    return vector * lax.rsqrt(jnp.mean(vector * vector, axis=-1, keepdims=True) + EPS)


def tables(positions, width):
    half_width = width // 2
    frequency = THETA ** (-jnp.arange(half_width, dtype=jnp.float32) / half_width)
    angles = positions[:, None] * frequency[None, :]
    return (jnp.cos(angles), jnp.sin(angles))


def rotate(vector, cosine, sine_table):
    half_width = vector.shape[-1] // 2
    first_half = vector[..., :half_width]
    second = vector[..., half_width:]
    cos_b = cosine[:, None, :]
    sin_b = sine_table[:, None, :]
    return jnp.concatenate(
        [first_half * cos_b - second * sin_b, second * cos_b + first_half * sin_b], axis=-1
    )


def dot(left, right, left_dim=1, right_dim=0):
    return lax.dot_general(
        left, right, (((left_dim,), (right_dim,)), ((), ())), preferred_element_type=jnp.float32
    )


def per_device(
    hidden_in,
    w_query,
    key_weight,
    value_weight,
    w_out,
    w_gate,
    w_up,
    w_down,
    norm_gains,
    head_gains,
    cotangent,
):
    low = jnp.bfloat16
    gain_block = jnp.zeros((SHARD_ROWS, 128), low)
    gain_block = gain_block.at[:, 0:2].set(norm_gains.T).at[0:4, 2:4].set(head_gains.T)
    pieces = [w_query, key_weight, value_weight, w_out.T, gain_block, w_gate, w_up, w_down.T]
    edges = [0]
    for piece in pieces:
        edges.append(edges[-1] + piece.shape[1])
    cuts = [(edges[i], edges[i + 1]) for i in range(len(pieces))]
    chunks = ((0, edges[5]), cuts[5], cuts[6], cuts[7])
    full = gather_weights(jnp.concatenate(pieces, axis=1), chunks)
    wq_full, wk_full, wv_full, wo_turned, gains_full, wg_full, wu_full, wd_turned = (
        full[:, lo:hi] for lo, hi in cuts
    )
    norm_gain = gains_full[:, 0:2].astype(jnp.float32).T
    head_gain = gains_full.reshape(16, SHARD_ROWS, 128)[:, 0:4, 2:4].reshape(HEAD_SIZE, 2)
    head_gain = head_gain.astype(jnp.float32).T

    tokens = hidden_in[0].astype(jnp.float32)
    token_count = tokens.shape[0]
    kv_local = wk_full.shape[1] // HEAD_SIZE
    q_local = wq_full.shape[1] // HEAD_SIZE
    groups = q_local // kv_local
    ctx = lax.axis_index("ctx")
    offset = ctx * token_count
    query_pos = offset + jnp.arange(token_count, dtype=jnp.int32)
    cosine, sine_table = tables(query_pos.astype(jnp.float32), HEAD_SIZE)

    def pre_norm(vector, gain):
        return rms_rows(vector) * gain

    def head_norm(raw, gain):
        return rotate(rms_rows(raw.reshape(token_count, -1, HEAD_SIZE)) * gain, cosine, sine_table)

    normalized_input = pre_norm(tokens, norm_gain[0]).astype(low)
    query_raw = dot(normalized_input, wq_full)
    key_unrotated = dot(normalized_input, wk_full)
    value_low = dot(normalized_input, wv_full).astype(low)
    query_low = head_norm(query_raw, head_gain[0]).astype(low)
    key_low = head_norm(key_unrotated, head_gain[1]).astype(low)
    grouped = query_low.reshape(token_count, kv_local, groups, HEAD_SIZE)
    packed = jnp.concatenate([key_low.reshape(token_count, kv_local * HEAD_SIZE), value_low], axis=1)
    other = ctx_swap(packed, 2)
    both = jnp.concatenate([other, packed], axis=0)
    seq_len = both.shape[0]
    keys_in = both[:, : kv_local * HEAD_SIZE].reshape(seq_len, kv_local, HEAD_SIZE)
    vals_in = both[:, kv_local * HEAD_SIZE :].reshape(seq_len, kv_local, HEAD_SIZE)
    other_pos = (1 - ctx) * token_count + jnp.arange(token_count, dtype=jnp.int32)
    key_pos = jnp.concatenate([other_pos, query_pos])
    visible = key_pos[None, :] <= query_pos[:, None]
    scores = (
        jnp.einsum("qkgd,skd->kgqs", grouped, keys_in, preferred_element_type=jnp.float32) * 0.125
    )
    weights = jnp.where(visible, jnp.exp(scores), 0.0)
    totals = jnp.sum(weights, axis=-1)
    accum = jnp.einsum(
        "kgqs,skd->kgqd", weights.astype(low), vals_in, preferred_element_type=jnp.float32
    )
    heads_out = accum / totals[..., None]
    attended_low = (
        jnp.transpose(heads_out, (2, 0, 1, 3)).reshape(token_count, q_local * HEAD_SIZE).astype(low)
    )
    branch = tp_total(dot(attended_low, wo_turned, 1, 1).astype(low), 3)
    residual = tokens + branch.astype(jnp.float32)
    mlp_in = pre_norm(residual, norm_gain[1]).astype(low)
    gate_proj = dot(mlp_in, wg_full)
    up_proj = dot(mlp_in, wu_full)
    sigma = jax.nn.sigmoid(gate_proj)
    silu_gate = gate_proj * sigma
    hidden_act = (silu_gate * up_proj).astype(low)
    mlp_part = dot(hidden_act, wd_turned, 1, 1)
    grad_top = cotangent[0]
    d_hidden = dot(grad_top, wd_turned)
    g_down = dot(grad_top, hidden_act, 0, 0)
    d_gate = (d_hidden * up_proj * sigma * (1.0 + gate_proj * (1.0 - sigma))).astype(low)
    d_up = (d_hidden * silu_gate).astype(low)
    g_gate = dot(mlp_in, d_gate, 0, 0)
    g_up = dot(mlp_in, d_up, 0, 0)
    d_mlp_part = dot(d_gate, wg_full, 1, 1) + dot(d_up, wu_full, 1, 1)
    sums = tp_total(jnp.concatenate([mlp_part.astype(low), d_mlp_part.astype(low)], axis=0), 4)
    block_out = (residual + sums[:token_count].astype(jnp.float32)).astype(low)
    unused_mlp, pull_mlp = jax.vjp(pre_norm, residual, norm_gain[1])
    d_resid_norm, g_gain_mlp = pull_mlp(sums[token_count:].astype(jnp.float32))
    d_residual = grad_top.astype(jnp.float32) + d_resid_norm
    d_branch = d_residual.astype(low)
    g_out = dot(d_branch, attended_low, 0, 0)
    d_attended = dot(d_branch, wo_turned).astype(low)
    d_grouped = d_attended.reshape(token_count, kv_local, groups, HEAD_SIZE)
    d_heads = jnp.transpose(d_grouped, (1, 2, 0, 3)).astype(jnp.float32)
    delta_row = jnp.sum(d_heads * heads_out, axis=-1)
    probs_now = weights / totals[..., None]
    d_probs = jnp.einsum("qkgd,skd->kgqs", d_grouped, vals_in, preferred_element_type=jnp.float32)
    d_scores = (probs_now * (d_probs - delta_row[..., None])).astype(low)
    d_query_acc = (
        jnp.einsum("kgqs,skd->kgqd", d_scores, keys_in, preferred_element_type=jnp.float32) * 0.125
    )
    d_keys = (
        jnp.einsum("kgqs,qkgd->skd", d_scores, grouped, preferred_element_type=jnp.float32) * 0.125
    )
    d_vals = jnp.einsum(
        "kgqs,qkgd->skd", probs_now.astype(low), d_grouped, preferred_element_type=jnp.float32
    )
    d_pack = jnp.concatenate(
        [
            d_keys.reshape(seq_len, kv_local * HEAD_SIZE),
            d_vals.reshape(seq_len, kv_local * HEAD_SIZE),
        ],
        axis=1,
    )
    d_other = ctx_swap(d_pack[:token_count].astype(low), 5)
    d_mine = (d_pack[token_count:] + d_other.astype(jnp.float32)).astype(low)
    d_key_low = d_mine[:, : kv_local * HEAD_SIZE]
    d_value_low = d_mine[:, kv_local * HEAD_SIZE :]
    d_query_low = (
        jnp.transpose(d_query_acc, (2, 0, 1, 3)).reshape(token_count, q_local, HEAD_SIZE).astype(low)
    )
    unused_query, pull_query = jax.vjp(head_norm, query_raw, head_gain[0])
    d_query_raw, g_head_query = pull_query(d_query_low.astype(jnp.float32))
    unused_key, pull_key = jax.vjp(head_norm, key_unrotated, head_gain[1])
    d_key_raw, g_head_key = pull_key(
        d_key_low.reshape(token_count, kv_local, HEAD_SIZE).astype(jnp.float32)
    )
    d_raw = jnp.concatenate([d_query_raw.astype(low), d_key_raw.astype(low), d_value_low], axis=1)
    g_raw = dot(normalized_input, d_raw, 0, 0)
    d_normed_part = dot(d_raw, full[:, 0 : cuts[2][1]], 1, 1)
    head_part = jnp.concatenate([g_head_query, g_head_key], axis=0).astype(low)
    head_rows = jnp.zeros((64, d_normed_part.shape[1]), low).at[0, 0:128].set(head_part)
    d_sums = tp_total(jnp.concatenate([d_normed_part.astype(low), head_rows], axis=0), 6)
    d_normed = d_sums[:token_count].astype(jnp.float32)
    g_head = d_sums[token_count, 0:128].reshape(2, HEAD_SIZE)
    unused_in, pull_in = jax.vjp(pre_norm, tokens, norm_gain[0])
    d_tokens_norm, g_gain_in = pull_in(d_normed)
    grad_in = d_residual + d_tokens_norm
    g_norm = jnp.stack([g_gain_in, g_gain_mlp], axis=1).astype(low)
    g_head = jnp.zeros((16, SHARD_ROWS, 2), low).at[:, 0:4].set(g_head.T.reshape(16, 4, 2))
    g_gains = jnp.concatenate(
        [g_norm, g_head.reshape(16 * SHARD_ROWS, 2), jnp.zeros((16 * SHARD_ROWS, 124), low)], axis=1
    )
    parts = jnp.concatenate(
        [
            g_raw.astype(low),
            g_out.astype(low),
            g_gains,
            g_gate.astype(low),
            g_up.astype(low),
            g_down.astype(low),
        ],
        axis=1,
    )
    mine = scatter_gradients(parts, chunks)
    r_query, r_key, r_value, r_out, r_gains, r_gate, r_up, r_down = (
        mine[:, lo:hi] for lo, hi in cuts
    )
    return (
        block_out[None],
        grad_in[None],
        r_query,
        r_key,
        r_value,
        r_out.T,
        r_gate,
        r_up,
        r_down.T,
        r_gains[:, 0:2].T,
        r_gains[0:4, 2:4].T,
    )


def solution(mesh):
    placed = (
        P("shard", "ctx", None),
        P("shard", "tp"),
        P("shard", "tp"),
        P("shard", "tp"),
        P("tp", "shard"),
        P("shard", "tp"),
        P("shard", "tp"),
        P("tp", "shard"),
        P(None, "shard"),
        P(None, "shard"),
        P("shard", "ctx", None),
    )
    return jax.shard_map(
        per_device,
        mesh=mesh,
        in_specs=placed,
        out_specs=(
            P("shard", "ctx", None),
            P("shard", "ctx", None),
            P("shard", "tp"),
            P("shard", "tp"),
            P("shard", "tp"),
            P("tp", "shard"),
            P("shard", "tp"),
            P("shard", "tp"),
            P("tp", "shard"),
            P(None, "shard"),
            P(None, "shard"),
        ),
        check_vma=False,
    )
```

```python
import jax
import jax.numpy as jnp
import numpy as np
from jax import lax
from jax.experimental import pallas as pl
from jax.experimental.pallas import tpu as pltpu
from jax.sharding import PartitionSpec as P

HEAD_SIZE = 64
EPS = 1e-05
THETA = 1000000.0
MESH = pl.DeviceIdType.MESH
VMEM_LIMIT = 62 * 1024 * 1024
HALF = 32
QUARTER = 16
SHARD_ROWS = 64


def ring_place():
    me = lax.axis_index("shard")
    return me // 4, lax.rem(me, 4)


def shard_at(z, y):
    return {"shard": lax.rem(z + 4, 4) * 4 + lax.rem(y + 4, 4)}


def greet(partners):
    barrier = pltpu.get_barrier_semaphore()
    for partner in partners:
        pl.semaphore_signal(barrier, inc=1, device_id=partner, device_id_type=MESH)
    pl.semaphore_wait(barrier, len(partners))


def remote(src, dst, send_sem, recv_sem, target):
    return pltpu.make_async_remote_copy(
        src_ref=src,
        dst_ref=dst,
        send_sem=send_sem,
        recv_sem=recv_sem,
        device_id=target,
        device_id_type=MESH,
    )


def torus_partners():
    z, y = ring_place()
    return [shard_at(z, y + 1), shard_at(z, y - 1), shard_at(z + 1, y), shard_at(z - 1, y)]


class Gather:

    def __init__(self, full, columns, send_sem, recv_sem, base):
        self.full = full
        self.columns = columns
        self.send_sem = send_sem
        self.recv_sem = recv_sem
        self.base = base
        self.z, self.y = ring_place()

    def rows(self, half, first, second, part):
        z, y = (self.z + second, self.y + first) if half == 0 else (self.z + first, self.y + second)
        block = lax.rem(z + 4, 4) * 4 + lax.rem(y + 4, 4)
        start = block * SHARD_ROWS + half * HALF + (QUARTER if part == 2 else 0)
        count = HALF if part == 0 else QUARTER
        lo, hi = self.columns
        return self.full.at[pl.ds(pl.multiple_of(start, QUARTER), count), lo:hi]

    def target(self, half, first, second):
        if half == 0:
            return shard_at(self.z + second, self.y + first)
        return shard_at(self.z + first, self.y + second)

    def copy(self, half, k, landed=False):
        if k < 4:
            step = (1, -1)[k % 2]
            if k < 2:
                sent, got = (0, 0, 0), (-step, 0, 0)
            else:
                sent, got = (-step, 0, 1 + k % 2), (-2 * step, 0, 1 + k % 2)
            target = (step, 0)
        else:
            j, kind = (k - 4) // 4, (k - 4) % 4
            offset = (0, -1, 1, 2)[j]
            step = (1, -1)[kind % 2]
            if kind < 2:
                sent, got = (offset, 0, 0), (offset, -step, 0)
            else:
                sent, got = (offset, -step, 1 + kind % 2), (offset, -2 * step, 1 + kind % 2)
            target = (0, step)
        index = self.base + half * 20 + k
        rows = self.rows(half, *(got if landed else sent))
        return remote(
            rows, rows, self.send_sem.at[index], self.recv_sem.at[index], self.target(half, *target)
        )

    def start(self, *ks):
        for k in ks:
            for half in (0, 1):
                self.copy(half, k).start()

    def arrived(self, *ks):
        for k in ks:
            for half in (0, 1):
                self.copy(half, k, True).wait_recv()

    def step(self, n):
        if n == 0:
            self.start(0, 1, 4, 5)
        elif n == 1:
            self.arrived(0)
            self.start(2, 8, 9)
            self.arrived(1)
            self.start(3, 12, 13)
        elif n == 2:
            self.arrived(4)
            self.start(6)
            self.arrived(5)
            self.start(7)
        elif n == 3:
            self.arrived(2, 3)
            self.start(16, 17)
        elif n == 4:
            for k in (8, 9, 12, 13, 16, 17):
                self.arrived(k)
                self.start(k + 2)
        elif n == 5:
            self.arrived(6, 7, 10, 11, 14, 15, 18, 19)

    def finish(self):
        for k in range(20):
            for half in (0, 1):
                self.copy(half, k).wait_send()


class Scatter:

    def __init__(self, part, landing, columns, send_sem, recv_sem, base):
        self.part = part
        self.landing = landing
        self.columns = columns
        self.send_sem = send_sem
        self.recv_sem = recv_sem
        self.base = base
        self.z, self.y = ring_place()

    def place(self, half, first, second):
        if half == 0:
            z, y = self.z + second, self.y + first
        else:
            z, y = self.z + first, self.y + second
        return lax.rem(z + 4, 4) * 4 + lax.rem(y + 4, 4)

    def rows(self, half, first, second, part):
        start = self.place(half, first, second) * SHARD_ROWS + half * HALF
        start = start + (QUARTER if part == 2 else 0)
        count = HALF if part == 0 else QUARTER
        lo, hi = self.columns
        return self.part.at[pl.ds(pl.multiple_of(start, QUARTER), count), lo:hi]

    def slot(self, half, j, kind):
        start = ((half * 5 + j) * 2) * 48 + (kind % 2) * 48 + (QUARTER if kind >= 2 else 0)
        count = HALF if kind >= 2 else QUARTER
        lo, hi = self.columns
        return self.landing.at[start : start + count, lo:hi]

    def copy(self, half, j, kind):
        step = (1, -1)[kind % 2]
        if kind < 2:
            along, part = 2, 1 + kind % 2
        else:
            along, part = step, 0
        if j < 4:
            offset = (2, -1, 1, 0)[j]
            src = self.rows(half, offset, along, part)
            target = {"shard": self.place(half, 0, step)}
        else:
            src = self.rows(half, along, 0, part)
            target = {"shard": self.place(half, step, 0)}
        index = self.base + (half * 5 + j) * 4 + kind
        return remote(src, self.slot(half, j, kind), self.send_sem.at[index], self.recv_sem.at[index], target)

    def add(self, half, target, *slots):
        total = target[...].astype(jnp.float32)
        for slot in slots:
            total = total + slot[...].astype(jnp.float32)
        target[...] = total.astype(jnp.bfloat16)

    def first(self, j):
        for half in (0, 1):
            for kind in (0, 1):
                self.copy(half, j, kind).start()

    def second(self, j):
        for kind in (0, 1):
            for half in (0, 1):
                self.copy(half, j, kind).wait_recv()
                step = (1, -1)[kind]
                if j < 4:
                    target = self.rows(half, (2, -1, 1, 0)[j], step, 1 + kind)
                else:
                    target = self.rows(half, step, 0, 1 + kind)
                self.add(half, target, self.slot(half, j, kind))
                self.copy(half, j, kind + 2).start()

    def third(self, j):
        for half in (0, 1):
            self.copy(half, j, 2).wait_recv()
            self.copy(half, j, 3).wait_recv()
            target = self.rows(half, (2, -1, 1, 0)[j] if j < 4 else 0, 0, 0)
            self.add(half, target, self.slot(half, j, 2), self.slot(half, j, 3))

    def finish(self):
        for half in (0, 1):
            for j in range(5):
                for kind in range(4):
                    self.copy(half, j, kind).wait_send()


def tp_place():
    me = lax.axis_index("tp")
    return me // 2, lax.rem(me, 2)


class TpSum:

    def __init__(self, part, landed, folded, out, send_sem, recv_sem, base):
        self.part, self.landed, self.folded, self.out = part, landed, folded, out
        self.send_sem, self.recv_sem, self.base = send_sem, recv_sem, base
        self.chip, self.core = tp_place()
        self.size = part.shape[0] // 4
        self.mine = self.block(self.chip, self.core)

    def block(self, chip, core):
        return pl.ds(pl.multiple_of((chip * 2 + core) * self.size, self.size), self.size)

    def copy(self, k):
        chip, core = self.chip, self.core
        if k == 0:
            src, dst = self.part.at[self.block(1 - chip, 1 - core)], self.landed.at[0]
        elif k == 1:
            src, dst = self.part.at[self.block(chip, 1 - core)], self.landed.at[1]
        elif k == 2:
            src, dst = self.folded, self.landed.at[2]
        elif k < 5:
            src = dst = self.out.at[self.mine]
        else:
            src = dst = self.out.at[self.block(1 - chip, core)]
        other_core = {"tp": chip * 2 + 1 - core}
        other_chip = {"tp": (1 - chip) * 2 + core}
        target = other_chip if k in (2, 3) else other_core
        return remote(src, dst, self.send_sem.at[self.base + k], self.recv_sem.at[self.base + k], target)

    def begin(self):
        self.copy(0).start()
        self.copy(1).start()

    def fold(self):
        self.copy(0).wait_recv()
        self.folded[...] = (
            self.part[self.block(1 - self.chip, self.core), :].astype(F32) + self.landed[0].astype(F32)
        ).astype(LOW)
        self.copy(2).start()

    def total(self):
        self.copy(1).wait_recv()
        self.copy(2).wait_recv()
        return (
            self.part[self.mine, :].astype(F32)
            + self.landed[1].astype(F32)
            + self.landed[2].astype(F32)
        )

    def back(self):
        self.copy(3).start()
        self.copy(4).start()

    def relay(self):
        self.copy(3).wait_recv()
        self.copy(5).start()

    def end(self):
        self.copy(4).wait_recv()
        self.copy(5).wait_recv()
        for k in range(6):
            self.copy(k).wait_send()


F32 = jnp.float32
LOW = jnp.bfloat16
TOKENS = 512
WIDTH = 1024
ROWS = 256
TILE = 384
TILES = 3
ATTN = 896
STRIDE = 3 * TILE
COLUMNS = ATTN + TILES * STRIDE
CHUNKS = ((0, ATTN),) + tuple((ATTN + STRIDE * t, ATTN + STRIDE * (t + 1)) for t in range(TILES))
SCORE_SCALE = 0.125 * 1.4426950408889634


def dot(left, right, left_dim=1, right_dim=0):
    return lax.dot_general(
        left, right, (((left_dim,), (right_dim,)), ((), ())), preferred_element_type=F32
    )


def iota(shape, dim):
    return lax.broadcasted_iota(jnp.int32, shape, dim)


def row_block(i, size=ROWS):
    return pl.ds(pl.multiple_of(i * size, size), size)


def loop(count, body):
    def step(i, carry):
        body(i)
        return carry

    lax.fori_loop(0, count, step, 0)


def split_dot(value, right):
    high = value.astype(LOW)
    low = (value - high.astype(F32)).astype(LOW)
    return dot(high, right) + dot(low, right)


def swap_halves(value):
    parts = []
    for at in range(0, value.shape[1], 128):
        part = value[:, at : at + 128]
        first = (iota(part.shape, 1) & 32) == 0
        parts.append(jnp.where(first, pltpu.roll(part, 96, 1), pltpu.roll(part, 32, 1)))
    return jnp.concatenate(parts, axis=1)


def wide(table):
    return jnp.concatenate([table, table, table], axis=1)


def to_key_lanes(blocks):
    first = iota(blocks[0].shape, 1) < 64
    zero = jnp.zeros_like(blocks[0])
    return [
        jnp.where(first, blocks[0], zero),
        jnp.where(first, pltpu.roll(blocks[0], 64, 1), zero),
        jnp.where(first, zero, pltpu.roll(blocks[1], 64, 1)),
        jnp.where(first, zero, blocks[1]),
    ]


def from_key_lanes(heads):
    first = iota(heads[0].shape, 1) < 64
    return jnp.concatenate(
        [
            jnp.where(first, heads[0], pltpu.roll(heads[1], 64, 1)),
            jnp.where(first, pltpu.roll(heads[2], 64, 1), heads[3]),
        ],
        axis=1,
    )


def block_kernel(
    hidden_hbm,
    cot_hbm,
    wq,
    wk,
    wv,
    wo,
    wg,
    wu,
    wd,
    norm_gains,
    head_gains,
    table_hbm,
    block_out,
    grad_in,
    out_query,
    out_key,
    out_value,
    out_wo,
    out_norm_gains,
    out_head_gains,
    out_gate,
    out_up,
    out_down,
    hidden,
    cot,
    table,
    w,
    grads,
    landing,
    other,
    normed,
    mlp_in,
    d_branch,
    probs,
    hid,
    dgu,
    q_heads,
    do_heads,
    o_heads,
    kv,
    att,
    attended,
    inverse,
    qk_norm,
    qk_scale,
    d_raw,
    kv_grad,
    kv_send,
    kv_got,
    res_own,
    d_res_own,
    inv_in,
    gain_rows,
    head_gain,
    gain_sums,
    head_mean,
    spread,
    part_a,
    part_b,
    landed,
    folded,
    gain_pass,
    gain_got,
    g_send,
    g_recv,
    s_send,
    s_recv,
    t_send,
    t_recv,
    c_send,
    c_recv,
    l_sem,
):
    me = lax.axis_index("shard")
    ctx = lax.axis_index("ctx")
    chip, core = tp_place()
    own = pl.ds(pl.multiple_of(me * SHARD_ROWS, SHARD_ROWS), SHARD_ROWS)
    ctx_peer = {"ctx": 1 - ctx}
    core_peer = {"tp": chip * 2 + 1 - core}
    chip_peer = {"tp": (1 - chip) * 2 + core}
    later = ctx.astype(F32)

    def weight_copy(k, src, at, count, start=0):
        src = src.at[:, start : start + count]
        return pltpu.make_async_copy(src, w.at[own, at : at + count], l_sem.at[k])

    first_copies = [
        weight_copy(0, wq, 0, 256),
        weight_copy(1, wk, 256, 128),
        weight_copy(2, wv, 384, 128),
        weight_copy(3, wo, 512, 256),
    ]
    tile_copies = [
        weight_copy(4 + 3 * t + k, src, ATTN + STRIDE * t + TILE * k, TILE, TILE * t)
        for t in range(TILES)
        for k, src in enumerate((wg, wu, wd))
    ]
    token_copies = [
        pltpu.make_async_copy(hidden_hbm, hidden, l_sem.at[13]),
        pltpu.make_async_copy(cot_hbm, cot, l_sem.at[14]),
        pltpu.make_async_copy(
            table_hbm.at[pl.ds(pl.multiple_of(ctx * TOKENS, TOKENS), TOKENS)], table, l_sem.at[15]
        ),
    ]
    for copy in first_copies + token_copies[:1] + tile_copies + token_copies[1:]:
        copy.start()
    eye = (iota((64, 64), 0) == iota((64, 64), 1)).astype(F32).astype(LOW)
    gain_sums[...] = jnp.zeros_like(gain_sums)
    gain_sums[0:2, 0:64] = norm_gains[...].astype(F32)
    gain_sums[2:4, 0:4] = head_gains[...].astype(F32)
    row = iota((128, 64), 0)
    block = jnp.zeros((128, 64), F32)
    for k in range(4):
        block = jnp.where(row == k, gain_sums[k : k + 1, 0:64], block)
    w[own, 768:896] = dot(eye, block.astype(LOW), 1, 1).astype(LOW)
    greet(torus_partners() + [ctx_peer, core_peer, chip_peer])
    gather = [Gather(w, chunk, g_send, g_recv, 40 * i) for i, chunk in enumerate(CHUNKS)]
    scatter = [Scatter(grads, landing, chunk, s_send, s_recv, 40 * i) for i, chunk in enumerate(CHUNKS)]
    for copy in first_copies:
        copy.wait()
    gather[0].step(0)

    head_mean[...] = jnp.where(
        (iota((384, 384), 0) // 64) == (iota((384, 384), 1) // 64), 1.0 / 64, 0.0
    ).astype(LOW)
    deep, lane = iota((WIDTH, 128), 0), iota((WIDTH, 128), 1)
    spread[...] = jnp.where(
        jnp.logical_and(deep % 64 < 4, (deep // 64) * 4 + deep % 64 == lane % 64), 1.0, 0.0
    ).astype(LOW)
    gain_sums[...] = jnp.zeros_like(gain_sums)
    kv[:, 256:384] = jnp.ones((2 * TOKENS, 128), LOW)
    for copy in tile_copies + token_copies:
        copy.wait()
    gather[0].step(1)

    def input_scale(i):
        x = hidden[row_block(i), :].astype(F32)
        inv_in[row_block(i), :] = lax.rsqrt(jnp.mean(x * x, axis=1, keepdims=True) + EPS)

    loop(2, input_scale)
    gather[0].step(2)
    gather[1].step(0)
    gather[0].step(3)
    gather[0].step(4)
    gather[0].step(5)
    gather[2].step(0)
    gather[1].step(1)

    pick = (iota((16, 128), 0) == iota((16, 128), 1)).astype(F32).astype(LOW)
    gain_rows[...] = dot(pick, w[:, 768:896], 1, 1)
    head_rows = dot(gain_rows[...].astype(LOW), spread[...])
    head_gain[...] = jnp.concatenate([head_rows[2:3], head_rows[2:3], head_rows[3:4]], axis=1)

    def angles(rows):
        return wide(table[rows, 0:128]), wide(table[rows, 128:256])

    def project(i):
        rows = row_block(i)
        x = hidden[rows, :].astype(F32) * inv_in[rows, :]
        low = (x * gain_rows[0:1, :]).astype(LOW)
        normed[rows, :] = low
        raw = dot(low, w[:, 0:512])
        qk = raw[:, 0:384]
        scale = lax.rsqrt(split_dot(qk * qk, head_mean[...]) + EPS)
        unit = qk * scale
        qk_norm[rows, :] = unit
        qk_scale[rows, :] = scale
        unit = unit * head_gain[...]
        cos, sin = angles(rows)
        turned = unit * cos + swap_halves(unit) * sin
        for h, head in enumerate(to_key_lanes([turned[:, 0:128], turned[:, 128:256]])):
            q_heads[h, rows, :] = head.astype(LOW)
        mine = pl.ds(pl.multiple_of(TOKENS + i * ROWS, ROWS), ROWS)
        kv[mine, 0:128] = turned[:, 256:384].astype(LOW)
        kv[mine, 128:256] = raw[:, 384:512].astype(LOW)

    loop(2, project)
    kv_copy = remote(
        kv.at[TOKENS : 2 * TOKENS, 0:256],
        kv.at[0:TOKENS, 0:256],
        c_send.at[0],
        c_recv.at[0],
        ctx_peer,
    )
    kv_copy.start()
    gather[1].step(2)
    gather[3].step(0)

    def attend_own(h):
        for i in range(2):
            rows, count = slice(ROWS * i, ROWS * (i + 1)), ROWS * (i + 1)
            keys = slice(TOKENS, TOKENS + count)
            scores = dot(q_heads[h, rows, :], kv[keys, 0:128], 1, 1)
            seen = iota(scores.shape, 1) <= iota(scores.shape, 0) + ROWS * i
            weights = jnp.where(seen, jnp.exp2(scores * SCORE_SCALE), 0.0).astype(LOW)
            probs[h, rows, keys] = weights
            o_heads[h, rows, :] = dot(weights, kv[keys, 128:384])

    def attend_other(h):
        for i in range(2):
            rows, keys = slice(ROWS * i, ROWS * (i + 1)), slice(0, TOKENS)
            scores = dot(q_heads[h, rows, :], kv[keys, 0:128], 1, 1)
            weights = (jnp.exp2(scores * SCORE_SCALE) * later).astype(LOW)
            probs[h, rows, keys] = weights
            o_heads[h, rows, :] += dot(weights, kv[keys, 128:384])

    loop(4, attend_own)
    gather[1].step(3)
    gather[2].step(1)
    kv_copy.wait()
    loop(4, attend_other)
    gather[1].step(4)
    gather[2].step(2)

    sums = [
        TpSum(part, landed.at[k], folded.at[k % 2], out, t_send, t_recv, 6 * k)
        for k, (part, out) in enumerate(
            ((part_a, mlp_in), (part_b, d_branch), (part_a, block_out), (part_b, grad_in))
        )
    ]
    mine = sums[0].mine

    def attended_rows(i):
        rows = row_block(i, 128)
        values = [o_heads[h, rows, :] for h in range(4)]
        scale = [1.0 / value[:, 128:256] for value in values]
        heads = from_key_lanes([value[:, 0:128] * s for value, s in zip(values, scale)])
        first = iota((128, 128), 1) < 64
        inverse[rows, :] = jnp.concatenate(
            [jnp.where(first, scale[0], scale[1]), jnp.where(first, scale[2], scale[3])], axis=1
        )
        att[rows, :] = heads
        attended[rows, :] = heads.astype(LOW)
        part_a[rows, :] = dot(heads.astype(LOW), w[:, 512:768], 1, 1).astype(LOW)

    loop(4, attended_rows)
    sums[0].begin()
    gather[1].step(5)
    sums[0].fold()
    gather[2].step(3)
    gather[3].step(1)
    residual = hidden[mine, :].astype(F32) + sums[0].total()
    res_scale = lax.rsqrt(jnp.mean(residual * residual, axis=1, keepdims=True) + EPS)
    res_own[...] = residual
    mlp_in[mine, :] = (residual * res_scale * gain_rows[1:2, :]).astype(LOW)
    sums[0].back()
    gather[2].step(4)
    gather[3].step(2)
    sums[0].relay()
    gather[3].step(3)
    sums[0].end()

    for t in range(TILES):
        at = ATTN + STRIDE * t
        if t == 1:
            gather[2].step(5)
            gather[3].step(4)
        if t == 2:
            gather[3].step(5)

        def feed(i):
            rows = row_block(i)
            both = dot(mlp_in[rows, :], w[:, at : at + 2 * TILE])
            gate, up = both[:, 0:TILE], both[:, TILE : 2 * TILE]
            sigma = jax.nn.sigmoid(gate)
            silu = gate * sigma
            hid[t, rows, :] = (silu * up).astype(LOW)
            d_hidden = dot(cot[rows, :], w[:, at + 2 * TILE : at + 3 * TILE])
            d_gate = d_hidden * up * sigma * (1.0 + gate * (1.0 - sigma))
            dgu[t, rows, 0:TILE] = d_gate.astype(LOW)
            dgu[t, rows, TILE : 2 * TILE] = (d_hidden * silu).astype(LOW)

        loop(2, feed)

    def mlp_back(n):
        rows = row_block(n)
        total = None
        for t in range(TILES):
            at = ATTN + STRIDE * t
            term = dot(dgu[t], w[rows, at : at + 2 * TILE], 1, 1)
            total = term if total is None else total + term
        part_b[:, rows] = total.astype(LOW)

    def mlp_out(n):
        rows = row_block(n)
        total = None
        for t in range(TILES):
            at = ATTN + STRIDE * t + 2 * TILE
            term = dot(hid[t], w[rows, at : at + TILE], 1, 1)
            total = term if total is None else total + term
        part_a[:, rows] = total.astype(LOW)

    def weight_grads(t):
        at = ATTN + STRIDE * t

        def rows_of(n):
            rows = row_block(n)
            grads[rows, at : at + 2 * TILE] = dot(mlp_in[:, rows], dgu[t], 0, 0).astype(LOW)
            grads[rows, at + 2 * TILE : at + 3 * TILE] = dot(cot[:, rows], hid[t], 0, 0).astype(LOW)

        loop(4, rows_of)
        for j in range(4):
            scatter[t + 1].first(j)

    loop(4, mlp_back)
    sums[1].begin()
    weight_grads(0)
    sums[1].fold()
    loop(4, mlp_out)
    sums[2].begin()
    weight_grads(1)
    residual = res_own[...]
    res_scale = lax.rsqrt(jnp.mean(residual * residual, axis=1, keepdims=True) + EPS)
    unit = residual * res_scale
    d_mlp_in = sums[1].total()
    gain_sums[1:2, :] = jnp.sum(d_mlp_in * unit, axis=0, keepdims=True)
    d_unit = d_mlp_in * gain_rows[1:2, :]
    d_res = cot[mine, :].astype(F32) + res_scale * (
        d_unit - unit * jnp.mean(d_unit * unit, axis=1, keepdims=True)
    )
    d_res_own[...] = d_res
    d_branch[mine, :] = d_res.astype(LOW)
    sums[1].back()
    sums[2].fold()
    weight_grads(2)
    sums[1].relay()
    for j in range(4):
        scatter[1].second(j)
    sums[1].end()
    block_out[mine, :] = (res_own[...] + sums[2].total()).astype(LOW)
    sums[2].back()

    def attended_back(i):
        rows = row_block(i)
        d_att = dot(d_branch[rows, :], w[:, 512:768]).astype(LOW).astype(F32)
        scaled = (d_att * inverse[rows, :]).astype(LOW).astype(F32)
        delta = -split_dot(scaled * att[rows, :], head_mean[0:256, 0:256])
        first = iota((ROWS, 128), 1) < 64
        moved = to_key_lanes([scaled[:, 0:128], scaled[:, 128:256]])
        for h in range(4):
            part = delta[:, 128 * (h // 2) : 128 * (h // 2 + 1)]
            high = part.astype(LOW).astype(F32)
            rest = pltpu.roll(part - high, 64, 1)
            do_heads[h, rows, 0:128] = moved[h].astype(LOW)
            do_heads[h, rows, 128:256] = (
                jnp.where(first, high, rest) if h % 2 == 0 else jnp.where(first, rest, high)
            ).astype(LOW)

    loop(2, attended_back)
    kv_grad[...] = jnp.zeros_like(kv_grad)

    def back_piece(h, rows, keys):
        weights = probs[h, rows, keys]
        d_probs = dot(do_heads[h, rows, :], kv[keys, 128:384], 1, 1)
        d_scores = (weights.astype(F32) * d_probs).astype(LOW)
        kv_grad[keys, 0:128] += dot(d_scores, q_heads[h, rows, :], 0, 0)
        kv_grad[keys, 128:256] += dot(weights, do_heads[h, rows, 0:128], 0, 0)
        return dot(d_scores, kv[keys, 0:128])

    def back_other(h):
        for i in range(2):
            rows = slice(ROWS * i, ROWS * (i + 1))
            o_heads[h, rows, 0:128] = back_piece(h, rows, slice(0, TOKENS))

    def back_own(h):
        for i in range(2):
            rows = slice(ROWS * i, ROWS * (i + 1))
            o_heads[h, rows, 0:128] += back_piece(h, rows, slice(TOKENS, TOKENS + ROWS * (i + 1)))

    loop(4, back_other)
    kv_send[:, 0:128] = (kv_grad[0:TOKENS, 0:128] * 0.125).astype(LOW)
    kv_send[:, 128:256] = kv_grad[0:TOKENS, 128:256].astype(LOW)
    kv_back = remote(kv_send, kv_got, c_send.at[1], c_recv.at[1], ctx_peer)
    kv_back.start()
    sums[2].relay()
    for j in range(4):
        scatter[2].second(j)
    for j in range(3):
        scatter[1].third(j)
    scatter[1].first(4)
    scatter[1].third(3)
    loop(4, back_own)
    for j in range(4):
        scatter[3].second(j)
    for j in range(3):
        scatter[2].third(j)
    scatter[2].first(4)
    scatter[2].third(3)
    scatter[1].second(4)
    sums[2].end()
    kv_back.wait()

    def raw_back(i):
        rows = row_block(i)
        dq = from_key_lanes([o_heads[h, rows, 0:128] for h in range(4)]) * 0.125
        mine_rows = pl.ds(pl.multiple_of(TOKENS + i * ROWS, ROWS), ROWS)
        got = kv_got[rows, :].astype(F32)
        dk = kv_grad[mine_rows, 0:128] * 0.125 + got[:, 0:128]
        d_raw[rows, 384:512] = (kv_grad[mine_rows, 128:256] + got[:, 128:256]).astype(LOW)
        turned = jnp.concatenate([dq, dk], axis=1).astype(LOW).astype(F32)
        cos, sin = angles(rows)
        d_out = turned * cos - swap_halves(turned) * sin
        unit = qk_norm[rows, :]
        gain_sums[4:5, 0:384] += jnp.sum(d_out * unit, axis=0, keepdims=True)
        d_unit = d_out * head_gain[...]
        inner = split_dot(d_unit * unit, head_mean[...])
        d_raw[rows, 0:384] = (qk_scale[rows, :] * (d_unit - unit * inner)).astype(LOW)

    loop(2, raw_back)

    def normed_back(i):
        rows = row_block(i)
        d_normed = dot(d_raw[rows, :], w[:, 0:512], 1, 1)
        unit = hidden[rows, :].astype(F32) * inv_in[rows, :]
        gain_sums[0:1, :] += jnp.sum(d_normed * unit, axis=0, keepdims=True)
        part_b[rows, :] = d_normed.astype(LOW)

    loop(2, normed_back)
    sums[3].begin()

    def attention_grads(n):
        rows = row_block(n)
        grads[rows, 0:512] = dot(normed[:, rows], d_raw[...], 0, 0).astype(LOW)
        grads[rows, 512:768] = dot(d_branch[:, rows], attended[...], 0, 0).astype(LOW)

    loop(4, attention_grads)
    heads = gain_sums[4:5, 0:384]
    head_row = iota((16, 128), 0)
    head_sums = jnp.where(
        head_row == 2,
        heads[:, 0:128] + heads[:, 128:256],
        jnp.where(head_row == 3, heads[:, 256:384], 0.0),
    )
    row = iota((16, WIDTH), 0)
    gain_all = jnp.where(
        row == 0,
        gain_sums[0:1, :],
        jnp.where(row == 1, gain_sums[1:2, :], dot(head_sums.astype(LOW), spread[...], 1, 1)),
    )
    grads[:, 768:896] = dot(gain_all.astype(LOW), pick, 0, 0).astype(LOW)
    for j in range(4):
        scatter[0].first(j)
    sums[3].fold()

    def swap_chunk(i):
        lo, hi = CHUNKS[i] if i else (0, 768)
        return remote(
            grads.at[own, lo:hi], other.at[:, lo:hi], c_send.at[2 + i], c_recv.at[2 + i], ctx_peer
        )

    for j in range(3):
        scatter[3].third(j)
    scatter[3].first(4)
    scatter[3].third(3)
    scatter[1].third(4)
    swap_chunk(1).start()
    scatter[2].second(4)
    for j in range(4):
        scatter[0].second(j)
    d_normed = sums[3].total()
    unit = hidden[mine, :].astype(F32) * inv_in[mine, :]
    d_unit = d_normed * gain_rows[0:1, :]
    grad_in[mine, :] = (
        d_res_own[...]
        + inv_in[mine, :] * (d_unit - unit * jnp.mean(d_unit * unit, axis=1, keepdims=True))
    ).astype(LOW)
    sums[3].back()
    for j in range(3):
        scatter[0].third(j)
    scatter[0].first(4)
    scatter[0].third(3)
    scatter[2].third(4)
    swap_chunk(2).start()
    scatter[3].second(4)
    scatter[0].second(4)
    sums[3].relay()
    scatter[3].third(4)
    swap_chunk(3).start()
    scatter[0].third(4)
    swap_chunk(0).start()

    def gain_copy(k, src, target):
        return remote(src, gain_got.at[k], c_send.at[6 + k], c_recv.at[6 + k], target)

    gain_pass[0] = grads[own, 768:896]
    passes = [
        gain_copy(k, gain_pass.at[k], target)
        for k, target in enumerate((core_peer, chip_peer, ctx_peer))
    ]
    for k in range(3):
        passes[k].start()
        passes[k].wait()
        if k < 2:
            total = gain_pass[k].astype(F32) + gain_got[k].astype(F32)
            gain_pass[k + 1] = total.astype(LOW)
        else:
            turned = dot(pick, gain_pass[k], 1, 1) + dot(pick, gain_got[k], 1, 1)
            out_norm_gains[...] = turned[0:2, :]
            out_head_gains[...] = turned[2:4, 0:4]

    def both_sums(lo, hi):
        return grads[own, lo:hi].astype(F32) + other[:, lo:hi].astype(F32)

    for t in range(TILES):
        swap_chunk(t + 1).wait()
        at, lanes = ATTN + STRIDE * t, slice(TILE * t, TILE * (t + 1))
        out_gate[:, lanes] = both_sums(at, at + TILE)
        out_up[:, lanes] = both_sums(at + TILE, at + 2 * TILE)
        out_down[:, lanes] = both_sums(at + 2 * TILE, at + 3 * TILE)
    swap_chunk(0).wait()
    out_query[...] = both_sums(0, 256)
    out_key[...] = both_sums(256, 384)
    out_value[...] = both_sums(384, 512)
    out_wo[...] = both_sums(512, 768)
    sums[3].end()
    for chunk in gather:
        chunk.finish()
    for chunk in scatter:
        chunk.finish()


def rotation_tables():
    frequency = THETA ** (-np.arange(32) / 32.0)
    angles = np.arange(2 * TOKENS)[:, None] * frequency[None, :]
    cosine, sine = np.cos(angles), np.sin(angles)
    return np.concatenate([cosine] * 4 + [-sine, sine] * 2, axis=1).astype(np.float32)


def per_device(
    hidden_in,
    w_query,
    key_weight,
    value_weight,
    w_out,
    w_gate,
    w_up,
    w_down,
    norm_gains,
    head_gains,
    cotangent,
):
    vmem = pl.BlockSpec(memory_space=pltpu.VMEM)
    hbm = pl.BlockSpec(memory_space=pl.ANY)

    def out(shape, dtype):
        return jax.ShapeDtypeStruct(shape, dtype)

    outs = [
        out((TOKENS, WIDTH), LOW),
        out((TOKENS, WIDTH), LOW),
        out((SHARD_ROWS, 256), F32),
        out((SHARD_ROWS, 128), F32),
        out((SHARD_ROWS, 128), F32),
        out((SHARD_ROWS, 256), F32),
        out((2, SHARD_ROWS), F32),
        out((2, 4), F32),
        out((SHARD_ROWS, TILE * TILES), F32),
        out((SHARD_ROWS, TILE * TILES), F32),
        out((SHARD_ROWS, TILE * TILES), F32),
    ]
    scratch = [
        pltpu.VMEM((TOKENS, WIDTH), LOW),
        pltpu.VMEM((TOKENS, WIDTH), LOW),
        pltpu.VMEM((TOKENS, 256), F32),
        pltpu.VMEM((WIDTH, COLUMNS), LOW),
        pltpu.VMEM((WIDTH, COLUMNS), LOW),
        pltpu.VMEM((960, COLUMNS), LOW),
        pltpu.VMEM((SHARD_ROWS, COLUMNS), LOW),
        pltpu.VMEM((TOKENS, WIDTH), LOW),
        pltpu.VMEM((TOKENS, WIDTH), LOW),
        pltpu.VMEM((TOKENS, WIDTH), LOW),
        pltpu.VMEM((4, TOKENS, 2 * TOKENS), LOW),
        pltpu.VMEM((TILES, TOKENS, TILE), LOW),
        pltpu.VMEM((TILES, TOKENS, 2 * TILE), LOW),
        pltpu.VMEM((4, TOKENS, 128), LOW),
        pltpu.VMEM((4, TOKENS, 256), LOW),
        pltpu.VMEM((4, TOKENS, 256), F32),
        pltpu.VMEM((2 * TOKENS, 384), LOW),
        pltpu.VMEM((TOKENS, 256), F32),
        pltpu.VMEM((TOKENS, 256), LOW),
        pltpu.VMEM((TOKENS, 256), F32),
        pltpu.VMEM((TOKENS, 384), F32),
        pltpu.VMEM((TOKENS, 384), F32),
        pltpu.VMEM((TOKENS, 512), LOW),
        pltpu.VMEM((2 * TOKENS, 256), F32),
        pltpu.VMEM((TOKENS, 256), LOW),
        pltpu.VMEM((TOKENS, 256), LOW),
        pltpu.VMEM((TOKENS // 4, WIDTH), F32),
        pltpu.VMEM((TOKENS // 4, WIDTH), F32),
        pltpu.VMEM((TOKENS, 1), F32),
        pltpu.VMEM((16, WIDTH), F32),
        pltpu.VMEM((1, 384), F32),
        pltpu.VMEM((8, WIDTH), F32),
        pltpu.VMEM((384, 384), LOW),
        pltpu.VMEM((WIDTH, 128), LOW),
        pltpu.VMEM((TOKENS, WIDTH), LOW),
        pltpu.VMEM((TOKENS, WIDTH), LOW),
        pltpu.VMEM((4, 3, TOKENS // 4, WIDTH), LOW),
        pltpu.VMEM((2, TOKENS // 4, WIDTH), LOW),
        pltpu.VMEM((3, SHARD_ROWS, 128), LOW),
        pltpu.VMEM((3, SHARD_ROWS, 128), LOW),
        pltpu.SemaphoreType.DMA((160,)),
        pltpu.SemaphoreType.DMA((160,)),
        pltpu.SemaphoreType.DMA((160,)),
        pltpu.SemaphoreType.DMA((160,)),
        pltpu.SemaphoreType.DMA((24,)),
        pltpu.SemaphoreType.DMA((24,)),
        pltpu.SemaphoreType.DMA((9,)),
        pltpu.SemaphoreType.DMA((9,)),
        pltpu.SemaphoreType.DMA((16,)),
    ]
    (
        block_out,
        grad_in,
        r_query,
        r_key,
        r_value,
        r_out,
        r_norm_gains,
        r_head_gains,
        r_gate,
        r_up,
        r_down,
    ) = pl.pallas_call(
        block_kernel,
        out_shape=outs,
        in_specs=[hbm] * 9 + [vmem] * 2 + [hbm],
        out_specs=[vmem] * 11,
        scratch_shapes=scratch,
        compiler_params=pltpu.CompilerParams(
            collective_id=0, has_side_effects=True, vmem_limit_bytes=VMEM_LIMIT
        ),
        name="transformer_block",
    )(
        hidden_in[0],
        cotangent[0],
        w_query,
        key_weight,
        value_weight,
        w_out.T,
        w_gate,
        w_up,
        w_down.T,
        norm_gains,
        head_gains,
        rotation_tables(),
    )
    return (
        block_out[None],
        grad_in.astype(F32)[None],
        r_query,
        r_key,
        r_value,
        r_out.T,
        r_gate,
        r_up,
        r_down.T,
        r_norm_gains,
        r_head_gains,
    )


def solution(mesh):
    placed = (
        P("shard", "ctx", None),
        P("shard", "tp"),
        P("shard", "tp"),
        P("shard", "tp"),
        P("tp", "shard"),
        P("shard", "tp"),
        P("shard", "tp"),
        P("tp", "shard"),
        P(None, "shard"),
        P(None, "shard"),
        P("shard", "ctx", None),
    )
    return jax.shard_map(
        per_device,
        mesh=mesh,
        in_specs=placed,
        out_specs=(
            P("shard", "ctx", None),
            P("shard", "ctx", None),
            P("shard", "tp"),
            P("shard", "tp"),
            P("shard", "tp"),
            P("tp", "shard"),
            P("shard", "tp"),
            P("shard", "tp"),
            P("tp", "shard"),
            P(None, "shard"),
            P(None, "shard"),
        ),
        check_vma=False,
    )
```

```python
import jax
import jax.numpy as jnp
import numpy as np
from jax import lax
from jax.experimental import pallas as pl
from jax.experimental.pallas import tpu as pltpu
from jax.sharding import PartitionSpec as P

HEAD_SIZE = 64
EPS = 1e-05
THETA = 1000000.0
MESH = pl.DeviceIdType.MESH
VMEM_LIMIT = 62 * 1024 * 1024
HALF = 32
QUARTER = 16
SHARD_ROWS = 64


def ring_place():
    me = lax.axis_index("shard")
    return me // 4, lax.rem(me, 4)


def shard_at(z, y):
    return {"shard": lax.rem(z + 4, 4) * 4 + lax.rem(y + 4, 4)}


def greet(partners):
    barrier = pltpu.get_barrier_semaphore()
    for partner in partners:
        pl.semaphore_signal(barrier, inc=1, device_id=partner, device_id_type=MESH)
    pl.semaphore_wait(barrier, len(partners))


def remote(src, dst, send_sem, recv_sem, target):
    return pltpu.make_async_remote_copy(
        src_ref=src,
        dst_ref=dst,
        send_sem=send_sem,
        recv_sem=recv_sem,
        device_id=target,
        device_id_type=MESH,
    )


def torus_partners():
    z, y = ring_place()
    return [shard_at(z, y + 1), shard_at(z, y - 1), shard_at(z + 1, y), shard_at(z - 1, y)]


class Gather:

    def __init__(self, full, columns, send_sem, recv_sem, base):
        self.full = full
        self.columns = columns
        self.send_sem = send_sem
        self.recv_sem = recv_sem
        self.base = base
        self.z, self.y = ring_place()

    def rows(self, half, first, second, part):
        z, y = (self.z + second, self.y + first) if half == 0 else (self.z + first, self.y + second)
        block = lax.rem(z + 4, 4) * 4 + lax.rem(y + 4, 4)
        start = block * SHARD_ROWS + half * HALF + (QUARTER if part == 2 else 0)
        count = HALF if part == 0 else QUARTER
        lo, hi = self.columns
        return self.full.at[pl.ds(pl.multiple_of(start, QUARTER), count), lo:hi]

    def target(self, half, first, second):
        if half == 0:
            return shard_at(self.z + second, self.y + first)
        return shard_at(self.z + first, self.y + second)

    def copy(self, half, k, landed=False):
        if k < 4:
            step = (1, -1)[k % 2]
            if k < 2:
                sent, got = (0, 0, 0), (-step, 0, 0)
            else:
                sent, got = (-step, 0, 1 + k % 2), (-2 * step, 0, 1 + k % 2)
            target = (step, 0)
        else:
            j, kind = (k - 4) // 4, (k - 4) % 4
            offset = (0, -1, 1, 2)[j]
            step = (1, -1)[kind % 2]
            if kind < 2:
                sent, got = (offset, 0, 0), (offset, -step, 0)
            else:
                sent, got = (offset, -step, 1 + kind % 2), (offset, -2 * step, 1 + kind % 2)
            target = (0, step)
        index = self.base + half * 20 + k
        rows = self.rows(half, *(got if landed else sent))
        return remote(
            rows, rows, self.send_sem.at[index], self.recv_sem.at[index], self.target(half, *target)
        )

    def start(self, *ks):
        for k in ks:
            for half in (0, 1):
                self.copy(half, k).start()

    def arrived(self, *ks):
        for k in ks:
            for half in (0, 1):
                self.copy(half, k, True).wait_recv()

    def step(self, n):
        if n == 0:
            self.start(0, 1, 4, 5)
        elif n == 1:
            self.arrived(0)
            self.start(2, 8, 9)
            self.arrived(1)
            self.start(3, 12, 13)
        elif n == 2:
            self.arrived(4)
            self.start(6)
            self.arrived(5)
            self.start(7)
        elif n == 3:
            self.arrived(2, 3)
            self.start(16, 17)
        elif n == 4:
            for k in (8, 9, 12, 13, 16, 17):
                self.arrived(k)
                self.start(k + 2)
        elif n == 5:
            self.arrived(6, 7, 10, 11, 14, 15, 18, 19)

    def finish(self):
        for k in range(20):
            for half in (0, 1):
                self.copy(half, k).wait_send()


class Scatter:

    def __init__(self, part, landing, columns, send_sem, recv_sem, base):
        self.part = part
        self.landing = landing
        self.columns = columns
        self.send_sem = send_sem
        self.recv_sem = recv_sem
        self.base = base
        self.z, self.y = ring_place()

    def place(self, half, first, second):
        if half == 0:
            z, y = self.z + second, self.y + first
        else:
            z, y = self.z + first, self.y + second
        return lax.rem(z + 4, 4) * 4 + lax.rem(y + 4, 4)

    def rows(self, half, first, second, part):
        start = self.place(half, first, second) * SHARD_ROWS + half * HALF
        start = start + (QUARTER if part == 2 else 0)
        count = HALF if part == 0 else QUARTER
        lo, hi = self.columns
        return self.part.at[pl.ds(pl.multiple_of(start, QUARTER), count), lo:hi]

    def slot(self, half, j, kind):
        start = ((half * 5 + j) * 2) * 48 + (kind % 2) * 48 + (QUARTER if kind >= 2 else 0)
        count = HALF if kind >= 2 else QUARTER
        lo, hi = self.columns
        return self.landing.at[start : start + count, lo:hi]

    def copy(self, half, j, kind):
        step = (1, -1)[kind % 2]
        if kind < 2:
            along, part = 2, 1 + kind % 2
        else:
            along, part = step, 0
        if j < 4:
            offset = (2, -1, 1, 0)[j]
            src = self.rows(half, offset, along, part)
            target = {"shard": self.place(half, 0, step)}
        else:
            src = self.rows(half, along, 0, part)
            target = {"shard": self.place(half, step, 0)}
        index = self.base + (half * 5 + j) * 4 + kind
        return remote(src, self.slot(half, j, kind), self.send_sem.at[index], self.recv_sem.at[index], target)

    def add(self, half, target, *slots):
        total = target[...].astype(jnp.float32)
        for slot in slots:
            total = total + slot[...].astype(jnp.float32)
        target[...] = total.astype(jnp.bfloat16)

    def first(self, j):
        for half in (0, 1):
            for kind in (0, 1):
                self.copy(half, j, kind).start()

    def second(self, j):
        for kind in (0, 1):
            for half in (0, 1):
                self.copy(half, j, kind).wait_recv()
                step = (1, -1)[kind]
                if j < 4:
                    target = self.rows(half, (2, -1, 1, 0)[j], step, 1 + kind)
                else:
                    target = self.rows(half, step, 0, 1 + kind)
                self.add(half, target, self.slot(half, j, kind))
                self.copy(half, j, kind + 2).start()

    def third(self, j):
        for half in (0, 1):
            self.copy(half, j, 2).wait_recv()
            self.copy(half, j, 3).wait_recv()
            target = self.rows(half, (2, -1, 1, 0)[j] if j < 4 else 0, 0, 0)
            self.add(half, target, self.slot(half, j, 2), self.slot(half, j, 3))

    def finish(self):
        for half in (0, 1):
            for j in range(5):
                for kind in range(4):
                    self.copy(half, j, kind).wait_send()


def tp_place():
    me = lax.axis_index("tp")
    return me // 2, lax.rem(me, 2)


class TpSum:

    def __init__(self, half, part, landed, folded, out, send_sem, recv_sem, base):
        self.half = half
        self.part, self.landed, self.folded, self.out = part, landed, folded, out
        self.send_sem, self.recv_sem, self.base = send_sem, recv_sem, base
        self.chip, self.core = tp_place()
        self.mine = self.block(self.chip, self.core)
        self.local = slice(half * SHARE, (half + 1) * SHARE)

    def block(self, chip, core):
        start = (chip * 2 + core) * 2 * SHARE + self.half * SHARE
        return pl.ds(pl.multiple_of(start, SHARE), SHARE)

    def copy(self, k):
        chip, core = self.chip, self.core
        if k == 0:
            src, dst = self.part.at[self.block(1 - chip, 1 - core)], self.landed.at[0]
        elif k == 1:
            src, dst = self.part.at[self.block(chip, 1 - core)], self.landed.at[1]
        elif k == 2:
            src, dst = self.folded, self.landed.at[2]
        elif k < 5:
            src = dst = self.out.at[self.mine]
        else:
            src = dst = self.out.at[self.block(1 - chip, core)]
        other_core = {"tp": chip * 2 + 1 - core}
        other_chip = {"tp": (1 - chip) * 2 + core}
        target = other_chip if k in (2, 3) else other_core
        return remote(src, dst, self.send_sem.at[self.base + k], self.recv_sem.at[self.base + k], target)

    def begin(self):
        self.copy(0).start()
        self.copy(1).start()

    def fold(self):
        self.copy(0).wait_recv()
        self.folded[...] = (
            self.part[self.block(1 - self.chip, self.core), :].astype(F32) + self.landed[0].astype(F32)
        ).astype(LOW)
        self.copy(2).start()

    def total(self):
        self.copy(1).wait_recv()
        self.copy(2).wait_recv()
        return (
            self.part[self.mine, :].astype(F32)
            + self.landed[1].astype(F32)
            + self.landed[2].astype(F32)
        )

    def back(self):
        self.copy(3).start()
        self.copy(4).start()

    def relay(self):
        self.copy(3).wait_recv()
        self.copy(5).start()

    def end(self):
        self.copy(4).wait_recv()
        self.copy(5).wait_recv()
        for k in range(6):
            self.copy(k).wait_send()


F32 = jnp.float32
LOW = jnp.bfloat16
TOKENS = 512
WIDTH = 1024
ROWS = 256
SHARE = 64
TILE = 384
TILES = 3
ATTN = 896
GAINS = 512
OUT = 640
STRIDE = 3 * TILE
COLUMNS = ATTN + TILES * STRIDE
CHUNKS = ((0, ATTN),) + tuple((ATTN + STRIDE * t, ATTN + STRIDE * (t + 1)) for t in range(TILES))
PARTS = ((0, OUT),) + tuple(
    (ATTN + STRIDE * t, ATTN + STRIDE * (t + 1)) for t in range(TILES)
) + ((OUT, ATTN),)
POLLS = {
    "scale": ((0, 2), (1, 0), (0, 3), (0, 4), (0, 5), (1, 1), (2, 0)),
    "own3": ((1, 2), (1, 3), (2, 1), (3, 0)),
    "fold": ((1, 4), (2, 2), (2, 3), (3, 1)),
    "back": ((1, 5), (2, 4), (3, 2), (3, 3)),
    "tile1": ((2, 5), (3, 4)),
    "tile2": ((3, 5),),
}
SUMS = {
    "begin1": ((1, 0),),
    "fold1": ((2, 0),),
    "grads": ((3, 0),),
    "back1": ((1, 1),),
    "outgrads": ((4, 0),),
    "other": ((2, 1),),
    "block": ((1, 2), (3, 1), (2, 2), (4, 1),),
    "fold3": ((1, 3), (3, 2), (0, 1), (4, 2), (2, 3),),
    "back3": ((0, 2), (3, 3), (1, 4), (0, 3), (2, 4),),
    "relay3": ((3, 4), (0, 4), (4, 3), (4, 4),),
}
SCORE_SCALE = 0.125 * 1.4426950408889634


def dot(left, right, left_dim=1, right_dim=0):
    return lax.dot_general(
        left, right, (((left_dim,), (right_dim,)), ((), ())), preferred_element_type=F32
    )


def iota(shape, dim):
    return lax.broadcasted_iota(jnp.int32, shape, dim)


def row_block(i, size=ROWS):
    return pl.ds(pl.multiple_of(i * size, size), size)


def loop(count, body):
    def step(i, carry):
        body(i)
        return carry

    lax.fori_loop(0, count, step, 0)


def split_dot(value, right):
    high = value.astype(LOW)
    low = (value - high.astype(F32)).astype(LOW)
    return dot(high, right) + dot(low, right)


def swap_halves(value):
    parts = []
    for at in range(0, value.shape[1], 128):
        part = value[:, at : at + 128]
        first = (iota(part.shape, 1) & 32) == 0
        parts.append(jnp.where(first, pltpu.roll(part, 96, 1), pltpu.roll(part, 32, 1)))
    return jnp.concatenate(parts, axis=1)


def wide(table):
    return jnp.concatenate([table, table, table], axis=1)


def to_key_lanes(blocks):
    first = iota(blocks[0].shape, 1) < 64
    zero = jnp.zeros_like(blocks[0])
    return [
        jnp.where(first, blocks[0], zero),
        jnp.where(first, pltpu.roll(blocks[0], 64, 1), zero),
        jnp.where(first, zero, pltpu.roll(blocks[1], 64, 1)),
        jnp.where(first, zero, blocks[1]),
    ]


def from_key_lanes(heads):
    first = iota(heads[0].shape, 1) < 64
    return jnp.concatenate(
        [
            jnp.where(first, heads[0], pltpu.roll(heads[1], 64, 1)),
            jnp.where(first, pltpu.roll(heads[2], 64, 1), heads[3]),
        ],
        axis=1,
    )


def block_kernel(
    hidden_hbm,
    cot_hbm,
    wq,
    wk,
    wv,
    wo,
    wg,
    wu,
    wd,
    norm_gains,
    head_gains,
    table_hbm,
    block_out_hbm,
    grad_in_hbm,
    query_hbm,
    key_hbm,
    value_hbm,
    wo_hbm,
    out_norm_gains,
    out_head_gains,
    gate_hbm,
    up_hbm,
    down_hbm,
    block_out,
    grad_in,
    out_query,
    out_key,
    out_value,
    out_wo,
    out_gate,
    out_up,
    out_down,
    hidden,
    cot,
    table,
    w,
    grads,
    landing,
    other,
    normed,
    mlp_in,
    d_branch,
    probs,
    hid,
    dgu,
    q_heads,
    do_heads,
    o_heads,
    kv,
    att,
    attended,
    inverse,
    qk_norm,
    qk_scale,
    d_raw,
    kv_grad,
    kv_send,
    kv_got,
    res_own,
    d_res_own,
    inv_in,
    gain_rows,
    head_gain,
    gain_sums,
    head_mean,
    spread,
    part_a,
    part_b,
    landed,
    folded,
    gain_got,
    g_send,
    g_recv,
    s_send,
    s_recv,
    t_send,
    t_recv,
    c_send,
    c_recv,
    l_sem,
    o_sem,
):
    me = lax.axis_index("shard")
    ctx = lax.axis_index("ctx")
    chip, core = tp_place()
    own = pl.ds(pl.multiple_of(me * SHARD_ROWS, SHARD_ROWS), SHARD_ROWS)
    ctx_peer = {"ctx": 1 - ctx}
    group = [
        {"ctx": lax.rem(ctx + k // 4, 2), "tp": lax.rem(chip * 2 + core + k % 4, 4)} for k in range(1, 8)
    ]
    partners = torus_partners() + group
    barrier = pltpu.get_barrier_semaphore()
    for partner in partners:
        pl.semaphore_signal(barrier, inc=1, device_id=partner, device_id_type=MESH)

    def weight_copy(k, src, at, count, start=0):
        src = src.at[:, start : start + count]
        return pltpu.make_async_copy(src, w.at[own, at : at + count], l_sem.at[k])

    first_copies = [
        weight_copy(0, wq, 0, 256),
        weight_copy(1, wk, 256, 128),
        weight_copy(2, wv, 384, 128),
        weight_copy(3, wo, OUT, 256),
    ]
    tile_copies = [
        weight_copy(4 + 3 * t + k, src, ATTN + STRIDE * t + TILE * k, TILE, TILE * t)
        for t in range(TILES)
        for k, src in enumerate((wg, wu, wd))
    ]
    token_copies = [
        pltpu.make_async_copy(hidden_hbm, hidden, l_sem.at[13]),
        pltpu.make_async_copy(cot_hbm, cot, l_sem.at[14]),
        pltpu.make_async_copy(
            table_hbm.at[pl.ds(pl.multiple_of(ctx * TOKENS, TOKENS), TOKENS)], table, l_sem.at[15]
        ),
    ]
    for copy in first_copies + token_copies[:1] + tile_copies + token_copies[1:]:
        copy.start()
    eye = (iota((64, 64), 0) == iota((64, 64), 1)).astype(F32).astype(LOW)
    gain_sums[...] = jnp.zeros_like(gain_sums)
    gain_sums[0:2, 0:64] = norm_gains[...].astype(F32)
    gain_sums[2:4, 0:4] = head_gains[...].astype(F32)
    row = iota((128, 64), 0)
    block = jnp.zeros((128, 64), F32)
    for k in range(4):
        block = jnp.where(row == k, gain_sums[k : k + 1, 0:64], block)
    w[own, GAINS:OUT] = dot(eye, block.astype(LOW), 1, 1).astype(LOW)
    gather = [Gather(w, chunk, g_send, g_recv, 40 * i) for i, chunk in enumerate(CHUNKS)]

    def scatter_step(i, step):
        part = scatter[i]
        if step == 0:
            for j in range(4):
                part.first(j)
        elif step == 1:
            for j in range(4):
                part.second(j)
        elif step == 2:
            for j in range(3):
                part.third(j)
            part.first(4)
            part.third(3)
        elif step == 3:
            part.second(4)
        else:
            part.third(4)
            swap_chunk(i).start()

    def swap_chunk(i):
        lo, hi = PARTS[i] if i else (0, GAINS)
        return remote(
            grads.at[own, lo:hi], other.at[:, lo:hi], c_send.at[4 + i], c_recv.at[4 + i], ctx_peer
        )

    def add_up(place):
        for part, step in SUMS.get(place, ()):
            scatter_step(part, step)

    def poll(place):
        for chunk, step in POLLS.get(place, ()):
            gather[chunk].step(step)

    scatter = [Scatter(grads, landing, part, s_send, s_recv, 40 * i) for i, part in enumerate(PARTS)]
    for copy in first_copies:
        copy.wait()
    pl.semaphore_wait(barrier, len(partners))
    gather[0].step(0)
    gather[0].step(1)

    head_mean[...] = jnp.where(
        (iota((384, 384), 0) // 64) == (iota((384, 384), 1) // 64), 1.0 / 64, 0.0
    ).astype(LOW)
    deep, lane = iota((WIDTH, 128), 0), iota((WIDTH, 128), 1)
    spread[...] = jnp.where(
        jnp.logical_and(deep % 64 < 4, (deep // 64) * 4 + deep % 64 == lane % 64), 1.0, 0.0
    ).astype(LOW)
    gain_sums[...] = jnp.zeros_like(gain_sums)
    kv[:, 256:384] = jnp.ones((2 * TOKENS, 128), LOW)

    def input_scale(i):
        x = hidden[row_block(i), :].astype(F32)
        inv_in[row_block(i), :] = lax.rsqrt(jnp.mean(x * x, axis=1, keepdims=True) + EPS)

    token_copies[0].wait()
    loop(2, input_scale)
    for copy in tile_copies:
        copy.wait()
    poll("scale")

    pick = (iota((16, 128), 0) == iota((16, 128), 1)).astype(F32).astype(LOW)
    gain_rows[...] = dot(pick, w[:, GAINS:OUT], 1, 1)
    head_rows = dot(gain_rows[...].astype(LOW), spread[...])
    head_gain[...] = jnp.concatenate([head_rows[2:3], head_rows[2:3], head_rows[3:4]], axis=1)

    def angles(rows):
        return wide(table[rows, 0:128]), wide(table[rows, 128:256])

    token_copies[2].wait()

    def project(i):
        rows = row_block(i)
        x = hidden[rows, :].astype(F32) * inv_in[rows, :]
        low = (x * gain_rows[0:1, :]).astype(LOW)
        normed[rows, :] = low
        raw = dot(low, w[:, 0:512])
        qk = raw[:, 0:384]
        scale = lax.rsqrt(split_dot(qk * qk, head_mean[...]) + EPS)
        unit = qk * scale
        qk_norm[rows, :] = unit
        qk_scale[rows, :] = scale
        unit = unit * head_gain[...]
        cos, sin = angles(rows)
        turned = unit * cos + swap_halves(unit) * sin
        for h, head in enumerate(to_key_lanes([turned[:, 0:128], turned[:, 128:256]])):
            q_heads[h, rows, :] = head.astype(LOW)
        mine = pl.ds(pl.multiple_of(TOKENS + i * ROWS, ROWS), ROWS)
        kv[mine, 0:128] = turned[:, 256:384].astype(LOW)
        kv[mine, 128:256] = raw[:, 384:512].astype(LOW)

    project(0)
    poll("project")
    project(1)
    def kv_copy(i):
        lanes = slice(128 * i, 128 * (i + 1))
        return remote(
            kv.at[TOKENS : 2 * TOKENS, lanes], kv.at[0:TOKENS, lanes], c_send.at[i], c_recv.at[i], ctx_peer
        )

    def kv_return(i):
        lanes = slice(128 * i, 128 * (i + 1))
        return remote(
            kv_send.at[:, lanes], kv_got.at[:, lanes], c_send.at[2 + i], c_recv.at[2 + i], ctx_peer
        )

    @pl.when(ctx == 0)
    def _():
        for i in range(2):
            kv_copy(i).start()
        kv[0:TOKENS, 0:256] = jnp.zeros((TOKENS, 256), LOW)


    def attend_own(h):
        for i in range(2):
            rows, count = slice(ROWS * i, ROWS * (i + 1)), ROWS * (i + 1)
            keys = slice(TOKENS, TOKENS + count)
            scores = dot(q_heads[h, rows, :], kv[keys, 0:128], 1, 1)
            seen = iota(scores.shape, 1) <= iota(scores.shape, 0) + ROWS * i
            weights = jnp.where(seen, jnp.exp2(scores * SCORE_SCALE), 0.0).astype(LOW)
            probs[h, rows, keys] = weights
            o_heads[h, rows, :] = dot(weights, kv[keys, 128:384])

    def attend_other(h):
        for i in range(2):
            rows, keys = slice(ROWS * i, ROWS * (i + 1)), slice(0, TOKENS)
            scores = dot(q_heads[h, rows, :], kv[keys, 0:128], 1, 1)
            weights = jnp.exp2(scores * SCORE_SCALE).astype(LOW)
            probs[h, rows, keys] = weights
            o_heads[h, rows, :] += dot(weights, kv[keys, 128:384])

    poll("keys")
    for h in range(4):
        attend_own(h)
        poll(f"own{h}")

    @pl.when(ctx == 1)
    def _():
        kv_copy(0).wait_recv()
        kv_copy(1).wait_recv()
        loop(2, attend_other)

    poll("other")

    @pl.when(ctx == 1)
    def _():
        loop(2, lambda h: attend_other(h + 2))

    poll("attended")

    sums = [
        [
            TpSum(half, part, landed.at[k, half], folded.at[k % 2, half], out, t_send, t_recv, 12 * k + 6 * half)
            for half in range(2)
        ]
        for k, (part, out) in enumerate(
            ((part_a, mlp_in), (part_b, d_branch), (part_a, block_out), (part_b, grad_in))
        )
    ]

    def each(k, *actions):
        for action in actions:
            for half in sums[k]:
                getattr(half, action)()

    def attended_rows(i):
        rows = row_block(i, 128)
        values = [o_heads[h, rows, :] for h in range(4)]
        scale = [1.0 / value[:, 128:256] for value in values]
        heads = from_key_lanes([value[:, 0:128] * s for value, s in zip(values, scale)])
        first = iota((128, 128), 1) < 64
        inverse[rows, :] = jnp.concatenate(
            [jnp.where(first, scale[0], scale[1]), jnp.where(first, scale[2], scale[3])], axis=1
        )
        att[rows, :] = heads
        attended[rows, :] = heads.astype(LOW)
        part_a[rows, :] = dot(heads.astype(LOW), w[:, OUT:ATTN], 1, 1).astype(LOW)

    loop(4, attended_rows)
    each(0, "begin")
    poll("begin")
    each(0, "fold")
    poll("fold")
    for half in sums[0]:
        residual = hidden[half.mine, :].astype(F32) + half.total()
        res_scale = lax.rsqrt(jnp.mean(residual * residual, axis=1, keepdims=True) + EPS)
        res_own[half.local, :] = residual
        mlp_in[half.mine, :] = (residual * res_scale * gain_rows[1:2, :]).astype(LOW)
        half.back()
    poll("back")
    each(0, "relay")
    poll("relay")
    each(0, "end")

    def weight_grads(t):
        at = ATTN + STRIDE * t

        def rows_of(n):
            rows = row_block(n)
            grads[rows, at : at + 2 * TILE] = dot(mlp_in[:, rows], dgu[t], 0, 0).astype(LOW)
            grads[rows, at + 2 * TILE : at + 3 * TILE] = dot(cot[:, rows], hid[t], 0, 0).astype(LOW)

        loop(4, rows_of)

    token_copies[1].wait()
    for t in range(TILES):
        at = ATTN + STRIDE * t
        poll(f"tile{t}")

        def feed(i):
            rows = row_block(i)
            both = dot(mlp_in[rows, :], w[:, at : at + 2 * TILE])
            gate, up = both[:, 0:TILE], both[:, TILE : 2 * TILE]
            sigma = jax.nn.sigmoid(gate)
            silu = gate * sigma
            hid[t, rows, :] = (silu * up).astype(LOW)
            d_hidden = dot(cot[rows, :], w[:, at + 2 * TILE : at + 3 * TILE])
            d_gate = d_hidden * up * sigma * (1.0 + gate * (1.0 - sigma))
            dgu[t, rows, 0:TILE] = d_gate.astype(LOW)
            dgu[t, rows, TILE : 2 * TILE] = (d_hidden * silu).astype(LOW)

        loop(2, feed)

    def mlp_back(n):
        rows = row_block(n)
        total = None
        for t in range(TILES):
            at = ATTN + STRIDE * t
            term = dot(dgu[t], w[rows, at : at + 2 * TILE], 1, 1)
            total = term if total is None else total + term
        part_b[:, rows] = total.astype(LOW)

    def mlp_out(n):
        rows = row_block(n)
        total = None
        for t in range(TILES):
            at = ATTN + STRIDE * t + 2 * TILE
            term = dot(hid[t], w[rows, at : at + TILE], 1, 1)
            total = term if total is None else total + term
        part_a[:, rows] = total.astype(LOW)

    loop(4, mlp_back)
    each(1, "begin")
    weight_grads(0)
    add_up("begin1")
    each(1, "fold")
    weight_grads(1)
    add_up("fold1")
    weight_grads(2)
    add_up("grads")
    gain_mlp = jnp.zeros((1, WIDTH), F32)
    for half in sums[1]:
        residual = res_own[half.local, :]
        res_scale = lax.rsqrt(jnp.mean(residual * residual, axis=1, keepdims=True) + EPS)
        unit = residual * res_scale
        d_mlp_in = half.total()
        gain_mlp += jnp.sum(d_mlp_in * unit, axis=0, keepdims=True)
        d_unit = d_mlp_in * gain_rows[1:2, :]
        d_res = cot[half.mine, :].astype(F32) + res_scale * (
            d_unit - unit * jnp.mean(d_unit * unit, axis=1, keepdims=True)
        )
        d_res_own[half.local, :] = d_res
        d_branch[half.mine, :] = d_res.astype(LOW)
        half.back()
    gain_sums[1:2, :] = gain_mlp
    loop(4, mlp_out)
    each(2, "begin")
    add_up("back1")
    each(1, "relay")
    each(1, "end")
    each(2, "fold")
    add_up("end1")

    def attended_back(i):
        rows = row_block(i)
        d_att = dot(d_branch[rows, :], w[:, OUT:ATTN]).astype(LOW).astype(F32)
        scaled = (d_att * inverse[rows, :]).astype(LOW).astype(F32)
        delta = -split_dot(scaled * att[rows, :], head_mean[0:256, 0:256])
        first = iota((ROWS, 128), 1) < 64
        moved = to_key_lanes([scaled[:, 0:128], scaled[:, 128:256]])
        for h in range(4):
            part = delta[:, 128 * (h // 2) : 128 * (h // 2 + 1)]
            high = part.astype(LOW).astype(F32)
            rest = pltpu.roll(part - high, 64, 1)
            do_heads[h, rows, 0:128] = moved[h].astype(LOW)
            do_heads[h, rows, 128:256] = (
                jnp.where(first, high, rest) if h % 2 == 0 else jnp.where(first, rest, high)
            ).astype(LOW)

    loop(2, attended_back)

    def out_grads(n):
        rows = row_block(n)
        grads[rows, OUT:ATTN] = dot(d_branch[:, rows], attended[...], 0, 0).astype(LOW)

    loop(4, out_grads)
    add_up("outgrads")
    kv_grad[...] = jnp.zeros_like(kv_grad)

    def back_piece(h, rows, keys):
        weights = probs[h, rows, keys]
        d_probs = dot(do_heads[h, rows, :], kv[keys, 128:384], 1, 1)
        d_scores = (weights.astype(F32) * d_probs).astype(LOW)
        kv_grad[keys, 0:128] += dot(d_scores, q_heads[h, rows, :], 0, 0)
        kv_grad[keys, 128:256] += dot(weights, do_heads[h, rows, 0:128], 0, 0)
        return dot(d_scores, kv[keys, 0:128])

    def back_other(h):
        for i in range(2):
            rows = slice(ROWS * i, ROWS * (i + 1))
            o_heads[h, rows, 0:128] = back_piece(h, rows, slice(0, TOKENS))

    def back_own(h):
        for i in range(2):
            rows = slice(ROWS * i, ROWS * (i + 1))
            o_heads[h, rows, 0:128] += back_piece(h, rows, slice(TOKENS, TOKENS + ROWS * (i + 1)))

    @pl.when(ctx == 1)
    def _():
        loop(4, back_other)
        kv_send[:, 0:128] = (kv_grad[0:TOKENS, 0:128] * 0.125).astype(LOW)
        kv_send[:, 128:256] = kv_grad[0:TOKENS, 128:256].astype(LOW)
        for i in range(2):
            kv_return(i).start()

    @pl.when(ctx == 0)
    def _():
        o_heads[:, :, 0:128] = jnp.zeros((4, TOKENS, 128), F32)

    add_up("other")
    loop(2, back_own)
    add_up("own1")
    loop(2, lambda h: back_own(h + 2))
    add_up("own3")
    for half in sums[2]:
        block_out[half.mine, :] = (res_own[half.local, :] + half.total()).astype(LOW)
        half.back()
    add_up("block")

    @pl.when(ctx == 0)
    def _():
        for i in range(2):
            kv_return(i).wait_recv()

    @pl.when(ctx == 1)
    def _():
        kv_got[...] = jnp.zeros_like(kv_got)

    def raw_back(i):
        rows = row_block(i)
        dq = from_key_lanes([o_heads[h, rows, 0:128] for h in range(4)]) * 0.125
        mine_rows = pl.ds(pl.multiple_of(TOKENS + i * ROWS, ROWS), ROWS)
        got = kv_got[rows, :].astype(F32)
        dk = kv_grad[mine_rows, 0:128] * 0.125 + got[:, 0:128]
        d_raw[rows, 384:512] = (kv_grad[mine_rows, 128:256] + got[:, 128:256]).astype(LOW)
        turned = jnp.concatenate([dq, dk], axis=1).astype(LOW).astype(F32)
        cos, sin = angles(rows)
        d_out = turned * cos - swap_halves(turned) * sin
        unit = qk_norm[rows, :]
        gain_sums[4:5, 0:384] += jnp.sum(d_out * unit, axis=0, keepdims=True)
        d_unit = d_out * head_gain[...]
        inner = split_dot(d_unit * unit, head_mean[...])
        d_raw[rows, 0:384] = (qk_scale[rows, :] * (d_unit - unit * inner)).astype(LOW)

    loop(2, raw_back)

    def normed_back(i):
        rows = row_block(i)
        d_normed = dot(d_raw[rows, :], w[:, 0:512], 1, 1)
        unit = hidden[rows, :].astype(F32) * inv_in[rows, :]
        gain_sums[0:1, :] += jnp.sum(d_normed * unit, axis=0, keepdims=True)
        part_b[rows, :] = d_normed.astype(LOW)

    loop(2, normed_back)
    each(3, "begin")

    def attention_grads(n):
        rows = row_block(n)
        grads[rows, 0:512] = dot(normed[:, rows], d_raw[...], 0, 0).astype(LOW)

    loop(4, attention_grads)
    heads = gain_sums[4:5, 0:384]
    head_row = iota((16, 128), 0)
    head_sums = jnp.where(
        head_row == 2,
        heads[:, 0:128] + heads[:, 128:256],
        jnp.where(head_row == 3, heads[:, 256:384], 0.0),
    )
    row = iota((16, WIDTH), 0)
    gain_all = jnp.where(
        row == 0,
        gain_sums[0:1, :],
        jnp.where(row == 1, gain_sums[1:2, :], dot(head_sums.astype(LOW), spread[...], 1, 1)),
    )
    grads[:, GAINS:OUT] = dot(gain_all.astype(LOW), pick, 0, 0).astype(LOW)
    scatter_step(0, 0)
    each(3, "fold")
    add_up("fold3")
    each(2, "relay")
    for half in sums[3]:
        rows = half.mine
        d_normed = half.total()
        unit = hidden[rows, :].astype(F32) * inv_in[rows, :]
        d_unit = d_normed * gain_rows[0:1, :]
        grad_in[rows, :] = (
            d_res_own[half.local, :]
            + inv_in[rows, :] * (d_unit - unit * jnp.mean(d_unit * unit, axis=1, keepdims=True))
        ).astype(LOW)
        half.back()
    add_up("back3")
    each(3, "relay")
    add_up("relay3")

    place = ctx * 4 + chip * 2 + core
    gain_got[place] = grads[own, GAINS:OUT]

    def gain_copy(k):
        return remote(
            grads.at[own, GAINS:OUT],
            gain_got.at[place],
            c_send.at[8 + k],
            c_recv.at[8 + k],
            group[k - 1],
        )

    for k in range(1, 8):
        gain_copy(k).start()

    written = []

    def write(source, target):
        copy = pltpu.make_async_copy(source, target, o_sem.at[len(written)])
        copy.start()
        written.append(copy)

    each(2, "end")
    write(block_out, block_out_hbm)

    def both_sums(lo, hi):
        return grads[own, lo:hi].astype(F32) + other[:, lo:hi].astype(F32)

    for t in range(TILES):
        swap_chunk(t + 1).wait()
        at, lanes = ATTN + STRIDE * t, slice(TILE * t, TILE * (t + 1))
        out_gate[:, lanes] = both_sums(at, at + TILE)
        out_up[:, lanes] = both_sums(at + TILE, at + 2 * TILE)
        out_down[:, lanes] = both_sums(at + 2 * TILE, at + 3 * TILE)
        for source, target in ((out_gate, gate_hbm), (out_up, up_hbm), (out_down, down_hbm)):
            write(source.at[:, lanes], target.at[:, lanes])
    swap_chunk(4).wait()
    out_wo[...] = both_sums(OUT, ATTN)
    write(out_wo, wo_hbm)
    each(3, "end")
    write(grad_in, grad_in_hbm)
    swap_chunk(0).wait()
    out_query[...] = both_sums(0, 256)
    out_key[...] = both_sums(256, 384)
    out_value[...] = both_sums(384, 512)
    write(out_query, query_hbm)
    write(out_key, key_hbm)
    write(out_value, value_hbm)
    turned = jnp.zeros((16, SHARD_ROWS), F32)
    for k in range(1, 8):
        gain_copy(k).wait()
    for k in range(8):
        turned = turned + dot(pick, gain_got[k], 1, 1)
    out_norm_gains[...] = turned[0:2, :]
    out_head_gains[...] = turned[2:4, 0:4]

    @pl.when(ctx == 0)
    def _():
        for i in range(2):
            kv_copy(i).wait_send()

    @pl.when(ctx == 1)
    def _():
        for i in range(2):
            kv_return(i).wait_send()

    for chunk in gather:
        chunk.finish()
    for chunk in scatter:
        chunk.finish()
    for copy in written:
        copy.wait()


def finish_kernel(norm_in, head_in, grad_low, *refs):
    sources, refs = refs[:8], refs[8:]
    norm_out, head_out, grad_out, targets, refs = refs[0], refs[1], refs[2], refs[3:11], refs[11:]
    low, full, held, refs = refs[0], refs[1], refs[2:10], refs[10:]
    load_sem, store_sem, low_sem, full_sem = refs
    pieces = [slice(128 * i, 128 * (i + 1)) for i in range(4)]
    grad_loads = [
        pltpu.make_async_copy(grad_low.at[p], low.at[p], low_sem.at[i]) for i, p in enumerate(pieces)
    ]
    grad_stores = [
        pltpu.make_async_copy(full.at[p], grad_out.at[p], full_sem.at[i]) for i, p in enumerate(pieces)
    ]
    loads = [pltpu.make_async_copy(a, b, load_sem.at[i]) for i, (a, b) in enumerate(zip(sources, held))]
    stores = [pltpu.make_async_copy(a, b, store_sem.at[i]) for i, (a, b) in enumerate(zip(held, targets))]
    for copy in grad_loads + loads:
        copy.start()
    norm_out[...] = norm_in[...]
    head_out[...] = head_in[...]
    for piece, load, store in zip(pieces, grad_loads, grad_stores):
        load.wait()
        full[piece, :] = low[piece, :].astype(F32)
        store.start()
    for load, store in zip(loads, stores):
        load.wait()
        store.start()
    for copy in stores + grad_stores:
        copy.wait()


def rotation_tables():
    frequency = THETA ** (-np.arange(32) / 32.0)
    angles = np.arange(2 * TOKENS)[:, None] * frequency[None, :]
    cosine, sine = np.cos(angles), np.sin(angles)
    return np.concatenate([cosine] * 4 + [-sine, sine] * 2, axis=1).astype(np.float32)


def per_device(
    hidden_in,
    w_query,
    key_weight,
    value_weight,
    w_out,
    w_gate,
    w_up,
    w_down,
    norm_gains,
    head_gains,
    cotangent,
):
    vmem = pl.BlockSpec(memory_space=pltpu.VMEM)
    hbm = pl.BlockSpec(memory_space=pl.ANY)

    def out(shape, dtype):
        return jax.ShapeDtypeStruct(shape, dtype)

    outs = [
        out((TOKENS, WIDTH), LOW),
        out((TOKENS, WIDTH), LOW),
        out((SHARD_ROWS, 256), F32),
        out((SHARD_ROWS, 128), F32),
        out((SHARD_ROWS, 128), F32),
        out((SHARD_ROWS, 256), F32),
        out((2, SHARD_ROWS), F32),
        out((2, 4), F32),
        out((SHARD_ROWS, TILE * TILES), F32),
        out((SHARD_ROWS, TILE * TILES), F32),
        out((SHARD_ROWS, TILE * TILES), F32),
    ]
    scratch = [
        pltpu.VMEM(value.shape, value.dtype) for k, value in enumerate(outs) if k not in (6, 7)
    ] + [
        pltpu.VMEM((TOKENS, WIDTH), LOW),
        pltpu.VMEM((TOKENS, WIDTH), LOW),
        pltpu.VMEM((TOKENS, 256), F32),
        pltpu.VMEM((WIDTH, COLUMNS), LOW),
        pltpu.VMEM((WIDTH, COLUMNS), LOW),
        pltpu.VMEM((960, COLUMNS), LOW),
        pltpu.VMEM((SHARD_ROWS, COLUMNS), LOW),
        pltpu.VMEM((TOKENS, WIDTH), LOW),
        pltpu.VMEM((TOKENS, WIDTH), LOW),
        pltpu.VMEM((TOKENS, WIDTH), LOW),
        pltpu.VMEM((4, TOKENS, 2 * TOKENS), LOW),
        pltpu.VMEM((TILES, TOKENS, TILE), LOW),
        pltpu.VMEM((TILES, TOKENS, 2 * TILE), LOW),
        pltpu.VMEM((4, TOKENS, 128), LOW),
        pltpu.VMEM((4, TOKENS, 256), LOW),
        pltpu.VMEM((4, TOKENS, 256), F32),
        pltpu.VMEM((2 * TOKENS, 384), LOW),
        pltpu.VMEM((TOKENS, 256), F32),
        pltpu.VMEM((TOKENS, 256), LOW),
        pltpu.VMEM((TOKENS, 256), F32),
        pltpu.VMEM((TOKENS, 384), F32),
        pltpu.VMEM((TOKENS, 384), F32),
        pltpu.VMEM((TOKENS, 512), LOW),
        pltpu.VMEM((2 * TOKENS, 256), F32),
        pltpu.VMEM((TOKENS, 256), LOW),
        pltpu.VMEM((TOKENS, 256), LOW),
        pltpu.VMEM((TOKENS // 4, WIDTH), F32),
        pltpu.VMEM((TOKENS // 4, WIDTH), F32),
        pltpu.VMEM((TOKENS, 1), F32),
        pltpu.VMEM((16, WIDTH), F32),
        pltpu.VMEM((1, 384), F32),
        pltpu.VMEM((8, WIDTH), F32),
        pltpu.VMEM((384, 384), LOW),
        pltpu.VMEM((WIDTH, 128), LOW),
        pltpu.VMEM((TOKENS, WIDTH), LOW),
        pltpu.VMEM((TOKENS, WIDTH), LOW),
        pltpu.VMEM((4, 2, 3, SHARE, WIDTH), LOW),
        pltpu.VMEM((2, 2, SHARE, WIDTH), LOW),
        pltpu.VMEM((8, SHARD_ROWS, 128), LOW),
        pltpu.SemaphoreType.DMA((200,)),
        pltpu.SemaphoreType.DMA((200,)),
        pltpu.SemaphoreType.DMA((200,)),
        pltpu.SemaphoreType.DMA((200,)),
        pltpu.SemaphoreType.DMA((48,)),
        pltpu.SemaphoreType.DMA((48,)),
        pltpu.SemaphoreType.DMA((16,)),
        pltpu.SemaphoreType.DMA((16,)),
        pltpu.SemaphoreType.DMA((16,)),
        pltpu.SemaphoreType.DMA((15,)),
    ]
    (
        block_out,
        grad_in,
        r_query,
        r_key,
        r_value,
        r_out,
        r_norm_gains,
        r_head_gains,
        r_gate,
        r_up,
        r_down,
    ) = pl.pallas_call(
        block_kernel,
        out_shape=outs,
        in_specs=[hbm] * 9 + [vmem] * 2 + [hbm],
        out_specs=[hbm] * 6 + [vmem] * 2 + [hbm] * 3,
        scratch_shapes=scratch,
        compiler_params=pltpu.CompilerParams(
            collective_id=0, has_side_effects=True, vmem_limit_bytes=VMEM_LIMIT
        ),
        name="transformer_block",
    )(
        hidden_in[0],
        cotangent[0],
        w_query,
        key_weight,
        value_weight,
        w_out.T,
        w_gate,
        w_up,
        w_down.T,
        norm_gains,
        head_gains,
        rotation_tables(),
    )
    plain = [block_out, r_query, r_key, r_value, r_out, r_gate, r_up, r_down]
    r_norm_gains, r_head_gains, grad_in, block_out, r_query, r_key, r_value, r_out, r_gate, r_up, r_down = (
        pl.pallas_call(
            finish_kernel,
            out_shape=[
                out(r_norm_gains.shape, F32),
                out(r_head_gains.shape, F32),
                out(grad_in.shape, F32),
            ]
            + [out(value.shape, value.dtype) for value in plain],
            in_specs=[vmem] * 2 + [hbm] * 9,
            out_specs=[vmem] * 2 + [hbm] * 9,
            scratch_shapes=[
                pltpu.VMEM((TOKENS, WIDTH), LOW),
                pltpu.VMEM((TOKENS, WIDTH), F32),
            ]
            + [pltpu.VMEM(value.shape, value.dtype) for value in plain]
            + [
                pltpu.SemaphoreType.DMA((8,)),
                pltpu.SemaphoreType.DMA((8,)),
                pltpu.SemaphoreType.DMA((4,)),
                pltpu.SemaphoreType.DMA((4,)),
            ],
            name="write_results",
        )(r_norm_gains, r_head_gains, grad_in, *plain)
    )
    return (
        block_out[None],
        grad_in[None],
        r_query,
        r_key,
        r_value,
        r_out.T,
        r_gate,
        r_up,
        r_down.T,
        r_norm_gains,
        r_head_gains,
    )


def solution(mesh):
    placed = (
        P("shard", "ctx", None),
        P("shard", "tp"),
        P("shard", "tp"),
        P("shard", "tp"),
        P("tp", "shard"),
        P("shard", "tp"),
        P("shard", "tp"),
        P("tp", "shard"),
        P(None, "shard"),
        P(None, "shard"),
        P("shard", "ctx", None),
    )
    return jax.shard_map(
        per_device,
        mesh=mesh,
        in_specs=placed,
        out_specs=(
            P("shard", "ctx", None),
            P("shard", "ctx", None),
            P("shard", "tp"),
            P("shard", "tp"),
            P("shard", "tp"),
            P("tp", "shard"),
            P("shard", "tp"),
            P("shard", "tp"),
            P("tp", "shard"),
            P(None, "shard"),
            P(None, "shard"),
        ),
        check_vma=False,
    )
```

```python
import jax
import jax.numpy as jnp
import numpy as np
from jax import lax
from jax.experimental import pallas as pl
from jax.experimental.pallas import tpu as pltpu
from jax.sharding import PartitionSpec as P

HEAD_SIZE = 64
EPS = 1e-05
THETA = 1000000.0
MESH = pl.DeviceIdType.MESH
VMEM_LIMIT = 62 * 1024 * 1024
HALF = 32
QUARTER = 16
SHARD_ROWS = 64


def ring_place():
    me = lax.axis_index("shard")
    return me // 4, lax.rem(me, 4)


def shard_at(z, y):
    return {"shard": lax.rem(z + 4, 4) * 4 + lax.rem(y + 4, 4)}


def greet(partners):
    barrier = pltpu.get_barrier_semaphore()
    for partner in partners:
        pl.semaphore_signal(barrier, inc=1, device_id=partner, device_id_type=MESH)
    pl.semaphore_wait(barrier, len(partners))


def remote(src, dst, send_sem, recv_sem, target):
    return pltpu.make_async_remote_copy(
        src_ref=src,
        dst_ref=dst,
        send_sem=send_sem,
        recv_sem=recv_sem,
        device_id=target,
        device_id_type=MESH,
    )


def torus_partners():
    z, y = ring_place()
    return [shard_at(z, y + 1), shard_at(z, y - 1), shard_at(z + 1, y), shard_at(z - 1, y)]


class Gather:

    def __init__(self, full, columns, send_sem, recv_sem, base):
        self.full = full
        self.columns = columns
        self.send_sem = send_sem
        self.recv_sem = recv_sem
        self.base = base
        self.z, self.y = ring_place()

    def rows(self, half, first, second, part):
        z, y = (self.z + second, self.y + first) if half == 0 else (self.z + first, self.y + second)
        block = lax.rem(z + 4, 4) * 4 + lax.rem(y + 4, 4)
        start = block * SHARD_ROWS + half * HALF + (QUARTER if part == 2 else 0)
        count = HALF if part == 0 else QUARTER
        lo, hi = self.columns
        return self.full.at[pl.ds(pl.multiple_of(start, QUARTER), count), lo:hi]

    def target(self, half, first, second):
        if half == 0:
            return shard_at(self.z + second, self.y + first)
        return shard_at(self.z + first, self.y + second)

    def copy(self, half, k, landed=False):
        if k < 4:
            step = (1, -1)[k % 2]
            if k < 2:
                sent, got = (0, 0, 0), (-step, 0, 0)
            else:
                sent, got = (-step, 0, 1 + k % 2), (-2 * step, 0, 1 + k % 2)
            target = (step, 0)
        else:
            j, kind = (k - 4) // 4, (k - 4) % 4
            offset = (0, -1, 1, 2)[j]
            step = (1, -1)[kind % 2]
            if kind < 2:
                sent, got = (offset, 0, 0), (offset, -step, 0)
            else:
                sent, got = (offset, -step, 1 + kind % 2), (offset, -2 * step, 1 + kind % 2)
            target = (0, step)
        index = self.base + half * 20 + k
        rows = self.rows(half, *(got if landed else sent))
        return remote(
            rows, rows, self.send_sem.at[index], self.recv_sem.at[index], self.target(half, *target)
        )

    def start(self, *ks):
        for k in ks:
            for half in (0, 1):
                self.copy(half, k).start()

    def arrived(self, *ks):
        for k in ks:
            for half in (0, 1):
                self.copy(half, k, True).wait_recv()

    def step(self, n):
        if n == 0:
            self.start(0, 1, 4, 5)
        elif n == 1:
            self.arrived(0)
            self.start(2, 8, 9)
            self.arrived(1)
            self.start(3, 12, 13)
        elif n == 2:
            self.arrived(4)
            self.start(6)
            self.arrived(5)
            self.start(7)
        elif n == 3:
            self.arrived(2, 3)
            self.start(16, 17)
        elif n == 4:
            for k in (8, 9, 12, 13, 16, 17):
                self.arrived(k)
                self.start(k + 2)
        elif n == 5:
            self.arrived(6, 7, 10, 11, 14, 15, 18, 19)

    def finish(self):
        for k in range(20):
            for half in (0, 1):
                self.copy(half, k).wait_send()


class Scatter:

    def __init__(self, part, landing, columns, send_sem, recv_sem, base):
        self.part = part
        self.landing = landing
        self.columns = columns
        self.send_sem = send_sem
        self.recv_sem = recv_sem
        self.base = base
        self.z, self.y = ring_place()

    def place(self, half, first, second):
        if half == 0:
            z, y = self.z + second, self.y + first
        else:
            z, y = self.z + first, self.y + second
        return lax.rem(z + 4, 4) * 4 + lax.rem(y + 4, 4)

    def rows(self, half, first, second, part):
        start = self.place(half, first, second) * SHARD_ROWS + half * HALF
        start = start + (QUARTER if part == 2 else 0)
        count = HALF if part == 0 else QUARTER
        lo, hi = self.columns
        return self.part.at[pl.ds(pl.multiple_of(start, QUARTER), count), lo:hi]

    def slot(self, half, j, kind):
        start = ((half * 5 + j) * 2) * 48 + (kind % 2) * 48 + (QUARTER if kind >= 2 else 0)
        count = HALF if kind >= 2 else QUARTER
        lo, hi = self.columns
        return self.landing.at[start : start + count, lo:hi]

    def copy(self, half, j, kind):
        step = (1, -1)[kind % 2]
        if kind < 2:
            along, part = 2, 1 + kind % 2
        else:
            along, part = step, 0
        if j < 4:
            offset = (2, -1, 1, 0)[j]
            src = self.rows(half, offset, along, part)
            target = {"shard": self.place(half, 0, step)}
        else:
            src = self.rows(half, along, 0, part)
            target = {"shard": self.place(half, step, 0)}
        index = self.base + (half * 5 + j) * 4 + kind
        return remote(src, self.slot(half, j, kind), self.send_sem.at[index], self.recv_sem.at[index], target)

    def add(self, half, target, *slots):
        total = target[...].astype(jnp.float32)
        for slot in slots:
            total = total + slot[...].astype(jnp.float32)
        target[...] = total.astype(jnp.bfloat16)

    def first(self, j):
        for half in (0, 1):
            for kind in (0, 1):
                self.copy(half, j, kind).start()

    def second(self, j):
        for kind in (0, 1):
            for half in (0, 1):
                self.copy(half, j, kind).wait_recv()
                step = (1, -1)[kind]
                if j < 4:
                    target = self.rows(half, (2, -1, 1, 0)[j], step, 1 + kind)
                else:
                    target = self.rows(half, step, 0, 1 + kind)
                self.add(half, target, self.slot(half, j, kind))
                self.copy(half, j, kind + 2).start()

    def third(self, j):
        for half in (0, 1):
            self.copy(half, j, 2).wait_recv()
            self.copy(half, j, 3).wait_recv()
            target = self.rows(half, (2, -1, 1, 0)[j] if j < 4 else 0, 0, 0)
            self.add(half, target, self.slot(half, j, 2), self.slot(half, j, 3))

    def finish(self):
        for half in (0, 1):
            for j in range(5):
                for kind in range(4):
                    self.copy(half, j, kind).wait_send()


def tp_place():
    me = lax.axis_index("tp")
    return me // 2, lax.rem(me, 2)


class TpSum:

    def __init__(self, half, part, landed, folded, out, send_sem, recv_sem, base):
        self.half = half
        self.part, self.landed, self.folded, self.out = part, landed, folded, out
        self.send_sem, self.recv_sem, self.base = send_sem, recv_sem, base
        self.chip, self.core = tp_place()
        self.mine = self.block(self.chip, self.core)
        self.local = slice(half * SHARE, (half + 1) * SHARE)

    def block(self, chip, core):
        start = (chip * 2 + core) * 2 * SHARE + self.half * SHARE
        return pl.ds(pl.multiple_of(start, SHARE), SHARE)

    def copy(self, k):
        chip, core = self.chip, self.core
        if k == 0:
            src, dst = self.part.at[self.block(1 - chip, 1 - core)], self.landed.at[0]
        elif k == 1:
            src, dst = self.part.at[self.block(chip, 1 - core)], self.landed.at[1]
        elif k == 2:
            src, dst = self.folded, self.landed.at[2]
        elif k < 5:
            src = dst = self.out.at[self.mine]
        else:
            src = dst = self.out.at[self.block(1 - chip, core)]
        other_core = {"tp": chip * 2 + 1 - core}
        other_chip = {"tp": (1 - chip) * 2 + core}
        target = other_chip if k in (2, 3) else other_core
        return remote(src, dst, self.send_sem.at[self.base + k], self.recv_sem.at[self.base + k], target)

    def begin(self):
        self.copy(0).start()
        self.copy(1).start()

    def fold(self):
        self.copy(0).wait_recv()
        self.folded[...] = (
            self.part[self.block(1 - self.chip, self.core), :].astype(F32) + self.landed[0].astype(F32)
        ).astype(LOW)
        self.copy(2).start()

    def total(self):
        self.copy(1).wait_recv()
        self.copy(2).wait_recv()
        return (
            self.part[self.mine, :].astype(F32)
            + self.landed[1].astype(F32)
            + self.landed[2].astype(F32)
        )

    def back(self):
        self.copy(3).start()
        self.copy(4).start()

    def relay(self):
        self.copy(3).wait_recv()
        self.copy(5).start()

    def end(self):
        self.copy(4).wait_recv()
        self.copy(5).wait_recv()
        for k in range(6):
            self.copy(k).wait_send()


F32 = jnp.float32
LOW = jnp.bfloat16
TOKENS = 512
WIDTH = 1024
ROWS = 256
SHARE = 64
TILE = 384
TILES = 3
ATTN = 896
GAINS = 512
OUT = 640
STRIDE = 3 * TILE
COLUMNS = ATTN + TILES * STRIDE
CHUNKS = ((0, ATTN),) + tuple((ATTN + STRIDE * t, ATTN + STRIDE * (t + 1)) for t in range(TILES))
PARTS = ((0, OUT),) + tuple(
    (ATTN + STRIDE * t, ATTN + STRIDE * (t + 1)) for t in range(TILES)
) + ((OUT, ATTN),)
POLLS = {
    "scale": ((0, 2), (1, 0), (0, 3), (0, 4), (0, 5), (1, 1), (2, 0)),
    "own3": ((1, 2), (1, 3), (2, 1), (3, 0)),
    "fold": ((1, 4), (2, 2), (2, 3), (3, 1)),
    "back": ((1, 5), (2, 4), (3, 2), (3, 3)),
    "tile1": ((2, 5), (3, 4)),
    "tile2": ((3, 5),),
}
SUMS = {
    "tile1": ((1, 0),),
    "fold1": ((2, 0),),
    "grads": ((3, 0),),
    "back1": ((1, 1),),
    "outgrads": ((4, 0),),
    "other": ((2, 1),),
    "block": ((1, 2), (3, 1), (2, 2), (4, 1),),
    "fold3": ((1, 3), (3, 2), (0, 1), (4, 2), (2, 3),),
    "back3": ((0, 2), (3, 3), (1, 4), (0, 3), (2, 4),),
    "relay3": ((3, 4), (0, 4), (4, 3), (4, 4),),
}
SCORE_SCALE = 0.125 * 1.4426950408889634


def dot(left, right, left_dim=1, right_dim=0):
    return lax.dot_general(
        left, right, (((left_dim,), (right_dim,)), ((), ())), preferred_element_type=F32
    )


def iota(shape, dim):
    return lax.broadcasted_iota(jnp.int32, shape, dim)


def row_block(i, size=ROWS):
    return pl.ds(pl.multiple_of(i * size, size), size)


def loop(count, body):
    def step(i, carry):
        body(i)
        return carry

    lax.fori_loop(0, count, step, 0)


def split_dot(value, right):
    high = value.astype(LOW)
    low = (value - high.astype(F32)).astype(LOW)
    return dot(high, right) + dot(low, right)


def swap_halves(value):
    parts = []
    for at in range(0, value.shape[1], 128):
        part = value[:, at : at + 128]
        first = (iota(part.shape, 1) & 32) == 0
        parts.append(jnp.where(first, pltpu.roll(part, 96, 1), pltpu.roll(part, 32, 1)))
    return jnp.concatenate(parts, axis=1)


def wide(table):
    return jnp.concatenate([table, table, table], axis=1)


def to_key_lanes(blocks):
    first = iota(blocks[0].shape, 1) < 64
    zero = jnp.zeros_like(blocks[0])
    return [
        jnp.where(first, blocks[0], zero),
        jnp.where(first, pltpu.roll(blocks[0], 64, 1), zero),
        jnp.where(first, zero, pltpu.roll(blocks[1], 64, 1)),
        jnp.where(first, zero, blocks[1]),
    ]


def from_key_lanes(heads):
    first = iota(heads[0].shape, 1) < 64
    return jnp.concatenate(
        [
            jnp.where(first, heads[0], pltpu.roll(heads[1], 64, 1)),
            jnp.where(first, pltpu.roll(heads[2], 64, 1), heads[3]),
        ],
        axis=1,
    )


def block_kernel(
    hidden_hbm,
    cot_hbm,
    wq,
    wk,
    wv,
    wo,
    wg,
    wu,
    wd,
    norm_gains,
    head_gains,
    table_hbm,
    block_out_hbm,
    grad_in_hbm,
    query_hbm,
    key_hbm,
    value_hbm,
    wo_hbm,
    out_norm_gains,
    out_head_gains,
    gate_hbm,
    up_hbm,
    down_hbm,
    block_out,
    grad_in,
    out_query,
    out_key,
    out_value,
    out_wo,
    out_gate,
    out_up,
    out_down,
    hidden,
    cot,
    table,
    w,
    grads,
    landing,
    other,
    normed,
    mlp_in,
    d_branch,
    probs,
    hid,
    dgu,
    q_heads,
    do_heads,
    o_heads,
    kv,
    att,
    attended,
    inverse,
    qk_norm,
    qk_scale,
    d_raw,
    kv_grad,
    kv_send,
    kv_got,
    res_own,
    d_res_own,
    inv_in,
    gain_rows,
    head_gain,
    gain_sums,
    head_mean,
    spread,
    part_a,
    part_b,
    landed,
    folded,
    gain_got,
    g_send,
    g_recv,
    s_send,
    s_recv,
    t_send,
    t_recv,
    c_send,
    c_recv,
    l_sem,
    o_sem,
):
    me = lax.axis_index("shard")
    ctx = lax.axis_index("ctx")
    chip, core = tp_place()
    own = pl.ds(pl.multiple_of(me * SHARD_ROWS, SHARD_ROWS), SHARD_ROWS)
    ctx_peer = {"ctx": 1 - ctx}
    group = [
        {"ctx": lax.rem(ctx + k // 4, 2), "tp": lax.rem(chip * 2 + core + k % 4, 4)} for k in range(1, 8)
    ]
    partners = torus_partners() + group
    barrier = pltpu.get_barrier_semaphore()
    for partner in partners:
        pl.semaphore_signal(barrier, inc=1, device_id=partner, device_id_type=MESH)

    def weight_copy(k, src, at, count, start=0):
        src = src.at[:, start : start + count]
        return pltpu.make_async_copy(src, w.at[own, at : at + count], l_sem.at[k])

    first_copies = [
        weight_copy(0, wq, 0, 256),
        weight_copy(1, wk, 256, 128),
        weight_copy(2, wv, 384, 128),
        weight_copy(3, wo, OUT, 256),
    ]
    tile_copies = [
        weight_copy(4 + 3 * t + k, src, ATTN + STRIDE * t + TILE * k, TILE, TILE * t)
        for t in range(TILES)
        for k, src in enumerate((wg, wu, wd))
    ]
    token_copies = [
        pltpu.make_async_copy(hidden_hbm, hidden, l_sem.at[13]),
        pltpu.make_async_copy(cot_hbm, cot, l_sem.at[14]),
        pltpu.make_async_copy(
            table_hbm.at[pl.ds(pl.multiple_of(ctx * TOKENS, TOKENS), TOKENS)], table, l_sem.at[15]
        ),
    ]
    for copy in first_copies + token_copies[:1] + tile_copies + token_copies[1:]:
        copy.start()
    eye = (iota((64, 64), 0) == iota((64, 64), 1)).astype(F32).astype(LOW)
    gain_sums[...] = jnp.zeros_like(gain_sums)
    gain_sums[0:2, 0:64] = norm_gains[...].astype(F32)
    gain_sums[2:4, 0:4] = head_gains[...].astype(F32)
    row = iota((128, 64), 0)
    block = jnp.zeros((128, 64), F32)
    for k in range(4):
        block = jnp.where(row == k, gain_sums[k : k + 1, 0:64], block)
    w[own, GAINS:OUT] = dot(eye, block.astype(LOW), 1, 1).astype(LOW)
    gather = [Gather(w, chunk, g_send, g_recv, 40 * i) for i, chunk in enumerate(CHUNKS)]

    def scatter_step(i, step):
        part = scatter[i]
        if step == 0:
            for j in range(4):
                part.first(j)
        elif step == 1:
            for j in range(4):
                part.second(j)
        elif step == 2:
            for j in range(3):
                part.third(j)
            part.first(4)
            part.third(3)
        elif step == 3:
            part.second(4)
        else:
            part.third(4)
            swap_chunk(i).start()

    def swap_chunk(i):
        lo, hi = PARTS[i] if i else (0, GAINS)
        return remote(
            grads.at[own, lo:hi], other.at[:, lo:hi], c_send.at[4 + i], c_recv.at[4 + i], ctx_peer
        )

    def add_up(place):
        for part, step in SUMS.get(place, ()):
            scatter_step(part, step)

    def poll(place):
        for chunk, step in POLLS.get(place, ()):
            gather[chunk].step(step)

    scatter = [Scatter(grads, landing, part, s_send, s_recv, 40 * i) for i, part in enumerate(PARTS)]
    for copy in first_copies:
        copy.wait()
    pl.semaphore_wait(barrier, len(partners))
    gather[0].step(0)
    gather[0].step(1)

    head_mean[...] = jnp.where(
        (iota((384, 384), 0) // 64) == (iota((384, 384), 1) // 64), 1.0 / 64, 0.0
    ).astype(LOW)
    deep, lane = iota((WIDTH, 128), 0), iota((WIDTH, 128), 1)
    spread[...] = jnp.where(
        jnp.logical_and(deep % 64 < 4, (deep // 64) * 4 + deep % 64 == lane % 64), 1.0, 0.0
    ).astype(LOW)
    gain_sums[...] = jnp.zeros_like(gain_sums)
    kv[:, 256:384] = jnp.ones((2 * TOKENS, 128), LOW)

    def input_scale(i):
        x = hidden[row_block(i), :].astype(F32)
        inv_in[row_block(i), :] = lax.rsqrt(jnp.mean(x * x, axis=1, keepdims=True) + EPS)

    token_copies[0].wait()
    loop(2, input_scale)
    for copy in tile_copies:
        copy.wait()
    poll("scale")

    pick = (iota((16, 128), 0) == iota((16, 128), 1)).astype(F32).astype(LOW)
    gain_rows[...] = dot(pick, w[:, GAINS:OUT], 1, 1)
    head_rows = dot(gain_rows[...].astype(LOW), spread[...])
    head_gain[...] = jnp.concatenate([head_rows[2:3], head_rows[2:3], head_rows[3:4]], axis=1)

    def angles(rows):
        return wide(table[rows, 0:128]), wide(table[rows, 128:256])

    token_copies[2].wait()

    def project(i):
        rows = row_block(i)
        x = hidden[rows, :].astype(F32) * inv_in[rows, :]
        low = (x * gain_rows[0:1, :]).astype(LOW)
        normed[rows, :] = low
        raw = dot(low, w[:, 0:512])
        qk = raw[:, 0:384]
        scale = lax.rsqrt(split_dot(qk * qk, head_mean[...]) + EPS)
        unit = qk * scale
        qk_norm[rows, :] = unit
        qk_scale[rows, :] = scale
        unit = unit * head_gain[...]
        cos, sin = angles(rows)
        turned = unit * cos + swap_halves(unit) * sin
        for h, head in enumerate(to_key_lanes([turned[:, 0:128], turned[:, 128:256]])):
            q_heads[h, rows, :] = head.astype(LOW)
        mine = pl.ds(pl.multiple_of(TOKENS + i * ROWS, ROWS), ROWS)
        kv[mine, 0:128] = turned[:, 256:384].astype(LOW)
        kv[mine, 128:256] = raw[:, 384:512].astype(LOW)

    project(0)
    poll("project")
    project(1)
    def kv_copy(i):
        lanes = slice(128 * i, 128 * (i + 1))
        return remote(
            kv.at[TOKENS : 2 * TOKENS, lanes], kv.at[0:TOKENS, lanes], c_send.at[i], c_recv.at[i], ctx_peer
        )

    def kv_return(i):
        lanes = slice(128 * i, 128 * (i + 1))
        return remote(
            kv_send.at[:, lanes], kv_got.at[:, lanes], c_send.at[2 + i], c_recv.at[2 + i], ctx_peer
        )

    @pl.when(ctx == 0)
    def _():
        for i in range(2):
            kv_copy(i).start()
        kv[0:TOKENS, 0:256] = jnp.zeros((TOKENS, 256), LOW)


    def attend_own(h):
        for i in range(2):
            rows, count = slice(ROWS * i, ROWS * (i + 1)), ROWS * (i + 1)
            keys = slice(TOKENS, TOKENS + count)
            scores = dot(q_heads[h, rows, :], kv[keys, 0:128], 1, 1)
            seen = iota(scores.shape, 1) <= iota(scores.shape, 0) + ROWS * i
            weights = jnp.where(seen, jnp.exp2(scores * SCORE_SCALE), 0.0).astype(LOW)
            probs[h, rows, keys] = weights
            o_heads[h, rows, :] = dot(weights, kv[keys, 128:384])

    def attend_other(h):
        for i in range(2):
            rows, keys = slice(ROWS * i, ROWS * (i + 1)), slice(0, TOKENS)
            scores = dot(q_heads[h, rows, :], kv[keys, 0:128], 1, 1)
            weights = jnp.exp2(scores * SCORE_SCALE).astype(LOW)
            probs[h, rows, keys] = weights
            o_heads[h, rows, :] += dot(weights, kv[keys, 128:384])

    poll("keys")
    for h in range(4):
        attend_own(h)
        poll(f"own{h}")

    @pl.when(ctx == 1)
    def _():
        kv_copy(0).wait_recv()
        kv_copy(1).wait_recv()
        loop(2, attend_other)

    poll("other")

    @pl.when(ctx == 1)
    def _():
        loop(2, lambda h: attend_other(h + 2))

    poll("attended")

    sums = [
        [
            TpSum(half, part, landed.at[k, half], folded.at[k % 2, half], out, t_send, t_recv, 12 * k + 6 * half)
            for half in range(2)
        ]
        for k, (part, out) in enumerate(
            ((part_a, mlp_in), (part_b, d_branch), (part_a, block_out), (part_b, grad_in))
        )
    ]

    def each(k, *actions):
        for action in actions:
            for half in sums[k]:
                getattr(half, action)()

    def attended_rows(i):
        rows = row_block(i, 128)
        values = [o_heads[h, rows, :] for h in range(4)]
        scale = [1.0 / value[:, 128:256] for value in values]
        heads = from_key_lanes([value[:, 0:128] * s for value, s in zip(values, scale)])
        first = iota((128, 128), 1) < 64
        inverse[rows, :] = jnp.concatenate(
            [jnp.where(first, scale[0], scale[1]), jnp.where(first, scale[2], scale[3])], axis=1
        )
        att[rows, :] = heads
        attended[rows, :] = heads.astype(LOW)
        part_a[rows, :] = dot(heads.astype(LOW), w[:, OUT:ATTN], 1, 1).astype(LOW)

    loop(4, attended_rows)
    each(0, "begin")
    poll("begin")
    each(0, "fold")
    poll("fold")
    for half in sums[0]:
        residual = hidden[half.mine, :].astype(F32) + half.total()
        res_scale = lax.rsqrt(jnp.mean(residual * residual, axis=1, keepdims=True) + EPS)
        res_own[half.local, :] = residual
        mlp_in[half.mine, :] = (residual * res_scale * gain_rows[1:2, :]).astype(LOW)
        half.back()
    poll("back")
    each(0, "relay")
    poll("relay")
    each(0, "end")

    def weight_grads(t):
        at = ATTN + STRIDE * t

        def rows_of(n):
            rows = row_block(n)
            grads[rows, at : at + 2 * TILE] = dot(mlp_in[:, rows], dgu[t], 0, 0).astype(LOW)
            grads[rows, at + 2 * TILE : at + 3 * TILE] = dot(cot[:, rows], hid[t], 0, 0).astype(LOW)

        loop(4, rows_of)

    token_copies[1].wait()
    for t in range(TILES):
        at = ATTN + STRIDE * t
        poll(f"tile{t}")

        def feed(i):
            rows = row_block(i)
            both = dot(mlp_in[rows, :], w[:, at : at + 2 * TILE])
            gate, up = both[:, 0:TILE], both[:, TILE : 2 * TILE]
            sigma = jax.nn.sigmoid(gate)
            silu = gate * sigma
            hid[t, rows, :] = (silu * up).astype(LOW)
            d_hidden = dot(cot[rows, :], w[:, at + 2 * TILE : at + 3 * TILE])
            d_gate = d_hidden * up * sigma * (1.0 + gate * (1.0 - sigma))
            dgu[t, rows, 0:TILE] = d_gate.astype(LOW)
            dgu[t, rows, TILE : 2 * TILE] = (d_hidden * silu).astype(LOW)

        loop(2, feed)
        if t == 1:
            weight_grads(0)
            add_up("tile1")

    def mlp_back(n):
        rows = row_block(n)
        total = None
        for t in range(TILES):
            at = ATTN + STRIDE * t
            term = dot(dgu[t], w[rows, at : at + 2 * TILE], 1, 1)
            total = term if total is None else total + term
        part_b[:, rows] = total.astype(LOW)

    def mlp_out(n):
        rows = row_block(n)
        total = None
        for t in range(TILES):
            at = ATTN + STRIDE * t + 2 * TILE
            term = dot(hid[t], w[rows, at : at + TILE], 1, 1)
            total = term if total is None else total + term
        part_a[:, rows] = total.astype(LOW)

    loop(4, mlp_back)
    each(1, "begin")
    each(1, "fold")
    weight_grads(1)
    add_up("fold1")
    weight_grads(2)
    add_up("grads")
    gain_mlp = jnp.zeros((1, WIDTH), F32)
    for half in sums[1]:
        residual = res_own[half.local, :]
        res_scale = lax.rsqrt(jnp.mean(residual * residual, axis=1, keepdims=True) + EPS)
        unit = residual * res_scale
        d_mlp_in = half.total()
        gain_mlp += jnp.sum(d_mlp_in * unit, axis=0, keepdims=True)
        d_unit = d_mlp_in * gain_rows[1:2, :]
        d_res = cot[half.mine, :].astype(F32) + res_scale * (
            d_unit - unit * jnp.mean(d_unit * unit, axis=1, keepdims=True)
        )
        d_res_own[half.local, :] = d_res
        d_branch[half.mine, :] = d_res.astype(LOW)
        half.back()
    gain_sums[1:2, :] = gain_mlp
    loop(4, mlp_out)
    each(2, "begin")
    add_up("back1")
    each(1, "relay")
    each(1, "end")
    each(2, "fold")
    add_up("end1")

    def attended_back(i):
        rows = row_block(i)
        d_att = dot(d_branch[rows, :], w[:, OUT:ATTN]).astype(LOW).astype(F32)
        scaled = (d_att * inverse[rows, :]).astype(LOW).astype(F32)
        delta = -split_dot(scaled * att[rows, :], head_mean[0:256, 0:256])
        first = iota((ROWS, 128), 1) < 64
        moved = to_key_lanes([scaled[:, 0:128], scaled[:, 128:256]])
        for h in range(4):
            part = delta[:, 128 * (h // 2) : 128 * (h // 2 + 1)]
            high = part.astype(LOW).astype(F32)
            rest = pltpu.roll(part - high, 64, 1)
            do_heads[h, rows, 0:128] = moved[h].astype(LOW)
            do_heads[h, rows, 128:256] = (
                jnp.where(first, high, rest) if h % 2 == 0 else jnp.where(first, rest, high)
            ).astype(LOW)

    loop(2, attended_back)

    def out_grads(n):
        rows = row_block(n)
        grads[rows, OUT:ATTN] = dot(d_branch[:, rows], attended[...], 0, 0).astype(LOW)

    loop(4, out_grads)
    add_up("outgrads")
    kv_grad[...] = jnp.zeros_like(kv_grad)

    def back_piece(h, rows, keys):
        weights = probs[h, rows, keys]
        d_probs = dot(do_heads[h, rows, :], kv[keys, 128:384], 1, 1)
        d_scores = (weights.astype(F32) * d_probs).astype(LOW)
        kv_grad[keys, 0:128] += dot(d_scores, q_heads[h, rows, :], 0, 0)
        kv_grad[keys, 128:256] += dot(weights, do_heads[h, rows, 0:128], 0, 0)
        return dot(d_scores, kv[keys, 0:128])

    def back_other(h):
        for i in range(2):
            rows = slice(ROWS * i, ROWS * (i + 1))
            o_heads[h, rows, 0:128] = back_piece(h, rows, slice(0, TOKENS))

    def back_own(h):
        for i in range(2):
            rows = slice(ROWS * i, ROWS * (i + 1))
            o_heads[h, rows, 0:128] += back_piece(h, rows, slice(TOKENS, TOKENS + ROWS * (i + 1)))

    @pl.when(ctx == 1)
    def _():
        loop(4, back_other)
        kv_send[:, 0:128] = (kv_grad[0:TOKENS, 0:128] * 0.125).astype(LOW)
        kv_send[:, 128:256] = kv_grad[0:TOKENS, 128:256].astype(LOW)
        for i in range(2):
            kv_return(i).start()

    @pl.when(ctx == 0)
    def _():
        o_heads[:, :, 0:128] = jnp.zeros((4, TOKENS, 128), F32)

    add_up("other")
    loop(2, back_own)
    add_up("own1")
    loop(2, lambda h: back_own(h + 2))
    add_up("own3")
    for half in sums[2]:
        block_out[half.mine, :] = (res_own[half.local, :] + half.total()).astype(LOW)
        half.back()
    add_up("block")

    @pl.when(ctx == 0)
    def _():
        for i in range(2):
            kv_return(i).wait_recv()

    @pl.when(ctx == 1)
    def _():
        kv_got[...] = jnp.zeros_like(kv_got)

    def raw_back(i):
        rows = row_block(i)
        dq = from_key_lanes([o_heads[h, rows, 0:128] for h in range(4)]) * 0.125
        mine_rows = pl.ds(pl.multiple_of(TOKENS + i * ROWS, ROWS), ROWS)
        got = kv_got[rows, :].astype(F32)
        dk = kv_grad[mine_rows, 0:128] * 0.125 + got[:, 0:128]
        d_raw[rows, 384:512] = (kv_grad[mine_rows, 128:256] + got[:, 128:256]).astype(LOW)
        turned = jnp.concatenate([dq, dk], axis=1).astype(LOW).astype(F32)
        cos, sin = angles(rows)
        d_out = turned * cos - swap_halves(turned) * sin
        unit = qk_norm[rows, :]
        gain_sums[4:5, 0:384] += jnp.sum(d_out * unit, axis=0, keepdims=True)
        d_unit = d_out * head_gain[...]
        inner = split_dot(d_unit * unit, head_mean[...])
        d_raw[rows, 0:384] = (qk_scale[rows, :] * (d_unit - unit * inner)).astype(LOW)

    loop(2, raw_back)

    def normed_back(i):
        rows = row_block(i)
        d_normed = dot(d_raw[rows, :], w[:, 0:512], 1, 1)
        unit = hidden[rows, :].astype(F32) * inv_in[rows, :]
        gain_sums[0:1, :] += jnp.sum(d_normed * unit, axis=0, keepdims=True)
        part_b[rows, :] = d_normed.astype(LOW)

    loop(2, normed_back)
    each(3, "begin")

    def attention_grads(n):
        rows = row_block(n)
        grads[rows, 0:512] = dot(normed[:, rows], d_raw[...], 0, 0).astype(LOW)

    loop(4, attention_grads)
    heads = gain_sums[4:5, 0:384]
    head_row = iota((16, 128), 0)
    head_sums = jnp.where(
        head_row == 2,
        heads[:, 0:128] + heads[:, 128:256],
        jnp.where(head_row == 3, heads[:, 256:384], 0.0),
    )
    row = iota((16, WIDTH), 0)
    gain_all = jnp.where(
        row == 0,
        gain_sums[0:1, :],
        jnp.where(row == 1, gain_sums[1:2, :], dot(head_sums.astype(LOW), spread[...], 1, 1)),
    )
    grads[:, GAINS:OUT] = dot(gain_all.astype(LOW), pick, 0, 0).astype(LOW)
    scatter_step(0, 0)
    each(3, "fold")
    add_up("fold3")
    each(2, "relay")
    for half in sums[3]:
        rows = half.mine
        d_normed = half.total()
        unit = hidden[rows, :].astype(F32) * inv_in[rows, :]
        d_unit = d_normed * gain_rows[0:1, :]
        grad_in[rows, :] = (
            d_res_own[half.local, :]
            + inv_in[rows, :] * (d_unit - unit * jnp.mean(d_unit * unit, axis=1, keepdims=True))
        ).astype(LOW)
        half.back()
    add_up("back3")
    each(3, "relay")
    add_up("relay3")

    place = ctx * 4 + chip * 2 + core
    gain_got[place] = grads[own, GAINS:OUT]

    def gain_copy(k):
        return remote(
            grads.at[own, GAINS:OUT],
            gain_got.at[place],
            c_send.at[8 + k],
            c_recv.at[8 + k],
            group[k - 1],
        )

    for k in range(1, 8):
        gain_copy(k).start()

    written = []

    def write(source, target):
        copy = pltpu.make_async_copy(source, target, o_sem.at[len(written)])
        copy.start()
        written.append(copy)

    each(2, "end")
    write(block_out, block_out_hbm)

    def both_sums(lo, hi):
        return grads[own, lo:hi].astype(F32) + other[:, lo:hi].astype(F32)

    for t in range(TILES):
        swap_chunk(t + 1).wait()
        at, lanes = ATTN + STRIDE * t, slice(TILE * t, TILE * (t + 1))
        out_gate[:, lanes] = both_sums(at, at + TILE)
        out_up[:, lanes] = both_sums(at + TILE, at + 2 * TILE)
        out_down[:, lanes] = both_sums(at + 2 * TILE, at + 3 * TILE)
        for source, target in ((out_gate, gate_hbm), (out_up, up_hbm), (out_down, down_hbm)):
            write(source.at[:, lanes], target.at[:, lanes])
    swap_chunk(4).wait()
    out_wo[...] = both_sums(OUT, ATTN)
    write(out_wo, wo_hbm)
    each(3, "end")
    write(grad_in, grad_in_hbm)
    swap_chunk(0).wait()
    out_query[...] = both_sums(0, 256)
    out_key[...] = both_sums(256, 384)
    out_value[...] = both_sums(384, 512)
    write(out_query, query_hbm)
    write(out_key, key_hbm)
    write(out_value, value_hbm)
    turned = jnp.zeros((16, SHARD_ROWS), F32)
    for k in range(1, 8):
        gain_copy(k).wait()
    for k in range(8):
        turned = turned + dot(pick, gain_got[k], 1, 1)
    out_norm_gains[...] = turned[0:2, :]
    out_head_gains[...] = turned[2:4, 0:4]

    @pl.when(ctx == 0)
    def _():
        for i in range(2):
            kv_copy(i).wait_send()

    @pl.when(ctx == 1)
    def _():
        for i in range(2):
            kv_return(i).wait_send()

    for chunk in gather:
        chunk.finish()
    for chunk in scatter:
        chunk.finish()
    for copy in written:
        copy.wait()


def finish_kernel(norm_in, head_in, grad_low, *refs):
    sources, refs = refs[:8], refs[8:]
    norm_out, head_out, grad_out, targets, refs = refs[0], refs[1], refs[2], refs[3:11], refs[11:]
    low, full, held, refs = refs[0], refs[1], refs[2:10], refs[10:]
    load_sem, store_sem, low_sem, full_sem = refs
    pieces = [slice(128 * i, 128 * (i + 1)) for i in range(4)]
    grad_loads = [
        pltpu.make_async_copy(grad_low.at[p], low.at[p], low_sem.at[i]) for i, p in enumerate(pieces)
    ]
    grad_stores = [
        pltpu.make_async_copy(full.at[p], grad_out.at[p], full_sem.at[i]) for i, p in enumerate(pieces)
    ]
    loads = [pltpu.make_async_copy(a, b, load_sem.at[i]) for i, (a, b) in enumerate(zip(sources, held))]
    stores = [pltpu.make_async_copy(a, b, store_sem.at[i]) for i, (a, b) in enumerate(zip(held, targets))]
    for copy in grad_loads + loads:
        copy.start()
    norm_out[...] = norm_in[...]
    head_out[...] = head_in[...]
    for piece, load, store in zip(pieces, grad_loads, grad_stores):
        load.wait()
        full[piece, :] = low[piece, :].astype(F32)
        store.start()
    for load, store in zip(loads, stores):
        load.wait()
        store.start()
    for copy in stores + grad_stores:
        copy.wait()


def rotation_tables():
    frequency = THETA ** (-np.arange(32) / 32.0)
    angles = np.arange(2 * TOKENS)[:, None] * frequency[None, :]
    cosine, sine = np.cos(angles), np.sin(angles)
    return np.concatenate([cosine] * 4 + [-sine, sine] * 2, axis=1).astype(np.float32)


def per_device(
    hidden_in,
    w_query,
    key_weight,
    value_weight,
    w_out,
    w_gate,
    w_up,
    w_down,
    norm_gains,
    head_gains,
    cotangent,
):
    vmem = pl.BlockSpec(memory_space=pltpu.VMEM)
    hbm = pl.BlockSpec(memory_space=pl.ANY)

    def out(shape, dtype):
        return jax.ShapeDtypeStruct(shape, dtype)

    outs = [
        out((TOKENS, WIDTH), LOW),
        out((TOKENS, WIDTH), LOW),
        out((SHARD_ROWS, 256), F32),
        out((SHARD_ROWS, 128), F32),
        out((SHARD_ROWS, 128), F32),
        out((SHARD_ROWS, 256), F32),
        out((2, SHARD_ROWS), F32),
        out((2, 4), F32),
        out((SHARD_ROWS, TILE * TILES), F32),
        out((SHARD_ROWS, TILE * TILES), F32),
        out((SHARD_ROWS, TILE * TILES), F32),
    ]
    scratch = [
        pltpu.VMEM(value.shape, value.dtype) for k, value in enumerate(outs) if k not in (6, 7)
    ] + [
        pltpu.VMEM((TOKENS, WIDTH), LOW),
        pltpu.VMEM((TOKENS, WIDTH), LOW),
        pltpu.VMEM((TOKENS, 256), F32),
        pltpu.VMEM((WIDTH, COLUMNS), LOW),
        pltpu.VMEM((WIDTH, COLUMNS), LOW),
        pltpu.VMEM((960, COLUMNS), LOW),
        pltpu.VMEM((SHARD_ROWS, COLUMNS), LOW),
        pltpu.VMEM((TOKENS, WIDTH), LOW),
        pltpu.VMEM((TOKENS, WIDTH), LOW),
        pltpu.VMEM((TOKENS, WIDTH), LOW),
        pltpu.VMEM((4, TOKENS, 2 * TOKENS), LOW),
        pltpu.VMEM((TILES, TOKENS, TILE), LOW),
        pltpu.VMEM((TILES, TOKENS, 2 * TILE), LOW),
        pltpu.VMEM((4, TOKENS, 128), LOW),
        pltpu.VMEM((4, TOKENS, 256), LOW),
        pltpu.VMEM((4, TOKENS, 256), F32),
        pltpu.VMEM((2 * TOKENS, 384), LOW),
        pltpu.VMEM((TOKENS, 256), F32),
        pltpu.VMEM((TOKENS, 256), LOW),
        pltpu.VMEM((TOKENS, 256), F32),
        pltpu.VMEM((TOKENS, 384), F32),
        pltpu.VMEM((TOKENS, 384), F32),
        pltpu.VMEM((TOKENS, 512), LOW),
        pltpu.VMEM((2 * TOKENS, 256), F32),
        pltpu.VMEM((TOKENS, 256), LOW),
        pltpu.VMEM((TOKENS, 256), LOW),
        pltpu.VMEM((TOKENS // 4, WIDTH), F32),
        pltpu.VMEM((TOKENS // 4, WIDTH), F32),
        pltpu.VMEM((TOKENS, 1), F32),
        pltpu.VMEM((16, WIDTH), F32),
        pltpu.VMEM((1, 384), F32),
        pltpu.VMEM((8, WIDTH), F32),
        pltpu.VMEM((384, 384), LOW),
        pltpu.VMEM((WIDTH, 128), LOW),
        pltpu.VMEM((TOKENS, WIDTH), LOW),
        pltpu.VMEM((TOKENS, WIDTH), LOW),
        pltpu.VMEM((4, 2, 3, SHARE, WIDTH), LOW),
        pltpu.VMEM((2, 2, SHARE, WIDTH), LOW),
        pltpu.VMEM((8, SHARD_ROWS, 128), LOW),
        pltpu.SemaphoreType.DMA((200,)),
        pltpu.SemaphoreType.DMA((200,)),
        pltpu.SemaphoreType.DMA((200,)),
        pltpu.SemaphoreType.DMA((200,)),
        pltpu.SemaphoreType.DMA((48,)),
        pltpu.SemaphoreType.DMA((48,)),
        pltpu.SemaphoreType.DMA((16,)),
        pltpu.SemaphoreType.DMA((16,)),
        pltpu.SemaphoreType.DMA((16,)),
        pltpu.SemaphoreType.DMA((15,)),
    ]
    (
        block_out,
        grad_in,
        r_query,
        r_key,
        r_value,
        r_out,
        r_norm_gains,
        r_head_gains,
        r_gate,
        r_up,
        r_down,
    ) = pl.pallas_call(
        block_kernel,
        out_shape=outs,
        in_specs=[hbm] * 9 + [vmem] * 2 + [hbm],
        out_specs=[hbm] * 6 + [vmem] * 2 + [hbm] * 3,
        scratch_shapes=scratch,
        compiler_params=pltpu.CompilerParams(
            collective_id=0, has_side_effects=True, vmem_limit_bytes=VMEM_LIMIT
        ),
        name="transformer_block",
    )(
        hidden_in[0],
        cotangent[0],
        w_query,
        key_weight,
        value_weight,
        w_out.T,
        w_gate,
        w_up,
        w_down.T,
        norm_gains,
        head_gains,
        rotation_tables(),
    )
    plain = [block_out, r_query, r_key, r_value, r_out, r_gate, r_up, r_down]
    r_norm_gains, r_head_gains, grad_in, block_out, r_query, r_key, r_value, r_out, r_gate, r_up, r_down = (
        pl.pallas_call(
            finish_kernel,
            out_shape=[
                out(r_norm_gains.shape, F32),
                out(r_head_gains.shape, F32),
                out(grad_in.shape, F32),
            ]
            + [out(value.shape, value.dtype) for value in plain],
            in_specs=[vmem] * 2 + [hbm] * 9,
            out_specs=[vmem] * 2 + [hbm] * 9,
            scratch_shapes=[
                pltpu.VMEM((TOKENS, WIDTH), LOW),
                pltpu.VMEM((TOKENS, WIDTH), F32),
            ]
            + [pltpu.VMEM(value.shape, value.dtype) for value in plain]
            + [
                pltpu.SemaphoreType.DMA((8,)),
                pltpu.SemaphoreType.DMA((8,)),
                pltpu.SemaphoreType.DMA((4,)),
                pltpu.SemaphoreType.DMA((4,)),
            ],
            name="write_results",
        )(r_norm_gains, r_head_gains, grad_in, *plain)
    )
    return (
        block_out[None],
        grad_in[None],
        r_query,
        r_key,
        r_value,
        r_out.T,
        r_gate,
        r_up,
        r_down.T,
        r_norm_gains,
        r_head_gains,
    )


def solution(mesh):
    placed = (
        P("shard", "ctx", None),
        P("shard", "tp"),
        P("shard", "tp"),
        P("shard", "tp"),
        P("tp", "shard"),
        P("shard", "tp"),
        P("shard", "tp"),
        P("tp", "shard"),
        P(None, "shard"),
        P(None, "shard"),
        P("shard", "ctx", None),
    )
    return jax.shard_map(
        per_device,
        mesh=mesh,
        in_specs=placed,
        out_specs=(
            P("shard", "ctx", None),
            P("shard", "ctx", None),
            P("shard", "tp"),
            P("shard", "tp"),
            P("shard", "tp"),
            P("tp", "shard"),
            P("shard", "tp"),
            P("shard", "tp"),
            P("tp", "shard"),
            P(None, "shard"),
            P(None, "shard"),
        ),
        check_vma=False,
    )
```
